32 devices in a mesh: ctx: 8 (over z, x), tp: 4 (over y, core).
Axes of the slice: x: 2, y: 2, z: 4, core: 2. Of those that a mesh axis runs over, the one named last changes fastest.
Arguments:
- out_gate: bfloat16 [1024, 8192], P('ctx', 'tp'), may hold values from -128 to 128
- key_proj: bfloat16 [1024, 8192], P('ctx', 'tp'), may hold values from -6 to 6
- value_proj: bfloat16 [1024, 8192], P('ctx', 'tp'), may hold values from -6 to 6
- residue: float32 [512, 16], P('tp'), may hold values from -1 to 1
- log_decay: float32 [512, 16], P('tp'), may hold values from -13 to -3
- skip: float32 [8192], P('tp'), may hold values from -4 to 4
- gain: float32 [8192], P('tp'), may hold values from 0.1 to 1.9
- cotangent: bfloat16 [1024, 8192], P('ctx', 'tp'), may hold values from -6 to 6
Outputs:
- mixer_out: bfloat16 [1024, 8192], P('ctx', 'tp')
- grad_q: bfloat16 [1024, 8192], P('ctx', 'tp')
- grad_k: bfloat16 [1024, 8192], P('ctx', 'tp')
- grad_v: bfloat16 [1024, 8192], P('ctx', 'tp')
- grad_residue: float32 [512, 16], P('tp')
- grad_log_decay: float32 [512, 16], P('tp')
The draws below stay inside these ranges and needn't reach their ends.
All inputs are finite; a program needn't handle non-finite values.
Results may differ from the reference program's by a relative error of at most 0.0013.
Values sent between devices are 32-bit elements; how exact they have to be, the bound alone decides.
A program may use at most 128 MiB of HBM per device.

```python
import math
import jax
import jax.numpy as jnp
from jax import lax

D = 8192
GROUP = 16
ORDER = 16
TOKENS = 1024


def mode_rates(key):
    pick_key, slow_key, fast_key = jax.random.split(jax.random.fold_in(key, 17), 3)
    shape = (D // GROUP, ORDER)
    slow = jnp.exp(jax.random.uniform(slow_key, shape, minval=math.log(0.3 / TOKENS), maxval=math.log(2.0 / TOKENS)))
    fast = jnp.exp(jax.random.uniform(fast_key, shape, minval=math.log(1.0 / 50.0), maxval=math.log(1.0 / 30.0)))
    share = 0.5
    chosen = jax.random.uniform(pick_key, shape) < share
    return jnp.where(chosen, slow, fast)


def draw_log_decay(key, part):
    return jnp.log(mode_rates(key)).astype(jnp.float32)


def draw_residue(key, part):
    rates = mode_rates(key)
    values = jax.random.truncated_normal(jax.random.fold_in(key, 29), -3.0, 3.0, rates.shape)
    return (values * jnp.sqrt(2.0 * rates)).astype(jnp.float32)


def draw_out_gate(key, part):
    base_key, row_key, col_key = jax.random.split(jax.random.fold_in(key, 3), 3)
    base = jax.random.truncated_normal(base_key, -4.0, 4.0, (TOKENS, D))
    rising = 0.5
    row_scale = 10.0 ** jax.random.uniform(row_key, (TOKENS, 1))
    channel_pos = jnp.arange(D, dtype=jnp.float32)[None, :] / D
    col_scale = 10.0 ** (rising * channel_pos + (1.0 - rising) * jax.random.uniform(col_key, (1, D)))
    return (0.3 * base * row_scale * col_scale).astype(jnp.bfloat16)


def block_scale(rng, shape, cuts, least, largest):
    level = 1.0
    for dim, parts in cuts:
        heights = jax.random.uniform(jax.random.fold_in(jax.random.fold_in(rng, 6), dim), (parts,), jnp.float32, least / len(cuts), largest / len(cuts))
        level = level * jnp.repeat(jnp.exp(heights), shape[dim] // parts).reshape((-1,) + (1,) * (len(shape) - 1 - dim))
    return level


def noise(own_key, dims, deviation, reach, cuts=(), held_as=jnp.bfloat16):
    factor_of = block_scale(own_key, dims, cuts, -0.22, 0.18) if cuts else 1.0
    values = jax.random.normal(own_key, dims, jnp.float32) * deviation * factor_of
    return jnp.minimum(jnp.maximum(values, -reach), reach).astype(held_as)


def setup_inputs(seed: int = 0) -> dict:
    keys = jax.random.split(jax.random.key(seed), 9)
    return {
        "out_gate": draw_out_gate(jax.random.fold_in(keys[8], 71), 0),
        "key_proj": noise(keys[1], (TOKENS, D), 1.0, 6.0, ((0, 8), (1, 4))),
        "value_proj": noise(keys[2], (TOKENS, D), 1.0, 6.0, ((0, 8), (1, 4))),
        "residue": draw_residue(jax.random.fold_in(keys[8], 71), 0),
        "log_decay": draw_log_decay(jax.random.fold_in(keys[8], 71), 0),
        "skip": noise(keys[5], (D,), 1.0, 4.0, ((0, 4),), jnp.float32),
        "gain": jnp.clip(1.0 + 0.18 * jax.random.normal(keys[6], (D,), jnp.float32), 0.1, 1.9),
        "cotangent": noise(keys[7], (TOKENS, D), 1.0, 6.0, ((0, 8), (1, 4))),
    }


EPSILON = 1e-06

def causal_conv(filter_taps, signal):
    seq_len = signal.shape[-1]
    padded_len = 2 * seq_len
    spectrum = jnp.fft.rfft(filter_taps, padded_len) * jnp.fft.rfft(signal, padded_len, axis=-1)
    return jnp.fft.irfft(spectrum, padded_len, axis=-1)[..., :seq_len]

def reference(out_gate, key_proj, value_proj, residue, log_decay, skip, gain, cotangent):
    seq_len, channel_count = out_gate.shape
    groups = residue.shape[0]
    gate_full = out_gate.astype(jnp.float32)
    key_full = key_proj.astype(jnp.float32)
    value_full = value_proj.astype(jnp.float32)
    signal = key_full * value_full
    decay_rate = jnp.exp(log_decay)
    lag_index = jnp.arange(seq_len, dtype=jnp.float32)

    def group_taps(residue_row, rate_row):
        return lax.optimization_barrier(jnp.sum(residue_row[:, None] * jnp.exp(-rate_row[:, None] * lag_index[None, :]), axis=0))
    signal_groups = signal.T.reshape(groups, GROUP, seq_len)

    def forward_group(inputs):
        residue_row, rate_row, group_signal = inputs
        return causal_conv(group_taps(residue_row, rate_row), group_signal)
    convolved = lax.map(forward_group, (residue, decay_rate, signal_groups)).reshape(channel_count, seq_len).T
    mixed = convolved + skip * signal
    premix = gate_full * mixed
    inverse = lax.rsqrt(lax.optimization_barrier(jnp.mean(premix * premix, axis=1, keepdims=True)) + EPSILON)
    normed = premix * inverse
    mixer_out = (normed * gain).astype(jnp.bfloat16)
    pull = cotangent.astype(jnp.float32) * gain
    dpre = (pull - normed * lax.optimization_barrier(jnp.mean(pull * normed, axis=1, keepdims=True))) * inverse
    grad_q = (dpre * mixed).astype(jnp.bfloat16)
    weight = dpre * gate_full
    grouped_weight_table = weight.T.reshape(groups, GROUP, seq_len)

    def backward_group(inputs):
        residue_row, rate_row, group_weight, group_signal = inputs
        filter_taps = group_taps(residue_row, rate_row)
        backward_part = jnp.flip(causal_conv(filter_taps, jnp.flip(group_weight, -1)), -1)
        padded_len = 2 * seq_len
        cross = jnp.fft.rfft(group_weight, padded_len, axis=-1) * jnp.conj(jnp.fft.rfft(group_signal, padded_len, axis=-1))
        lagged = lax.optimization_barrier(jnp.sum(jnp.fft.irfft(cross, padded_len, axis=-1)[:, :seq_len], axis=0))
        decay_table = jnp.exp(-rate_row[:, None] * lag_index[None, :])
        residue_grad = lax.optimization_barrier(jnp.sum(decay_table * lagged[None, :], axis=1))
        moment_grad = lax.optimization_barrier(jnp.sum(decay_table * lag_index[None, :] * lagged[None, :], axis=1))
        return (backward_part, residue_grad, -residue_row * rate_row * moment_grad)
    backward_part, residue_grad, decay_grad = lax.map(backward_group, (residue, decay_rate, grouped_weight_table, signal_groups))
    grad_signal = backward_part.reshape(channel_count, seq_len).T + skip * weight
    grad_k = (grad_signal * value_full).astype(jnp.bfloat16)
    grad_v = (grad_signal * key_full).astype(jnp.bfloat16)
    return (mixer_out, grad_q, grad_k, grad_v, residue_grad / seq_len, decay_grad / seq_len)
```

```python
import functools

import jax
import jax.numpy as jnp
from jax import lax
from jax.experimental import pallas as pl
from jax.experimental.pallas import tpu as pltpu
from jax.sharding import PartitionSpec as P

EPSILON = 1e-06
LANES = 128
SUB = 32
F32 = jnp.float32
BF16 = jnp.bfloat16
MESH = pl.DeviceIdType.MESH


def halves(value):
    high = value.astype(BF16)
    return high, (value - high.astype(F32)).astype(BF16)


def dot(a, b):
    return jnp.dot(a, b, preferred_element_type=F32)


def dot_t(a, b):
    return lax.dot_general(a, b, (((1,), (1,)), ((), ())), preferred_element_type=F32)


def product(left, right, multiply=dot):
    rows = left[0].shape[0]
    both = multiply(jnp.concatenate(left, axis=0), right[0])
    return both[:rows] + both[rows:] + multiply(left[0], right[1])


def exact_dot(value, ones):
    rows = value.shape[0]
    high, rest = value.astype(BF16), None
    rest = value - high.astype(F32)
    mid = rest.astype(BF16)
    low = (rest - mid.astype(F32)).astype(BF16)
    out = dot(jnp.concatenate([high, mid, low], axis=0), ones)
    return out[:rows] + out[rows : 2 * rows] + out[2 * rows :]


def iota(shape, dim):
    return lax.broadcasted_iota(jnp.int32, shape, dim)


def kernel(
    ctx_count,
    tp_count,
    full_width,
    modes,
    members,
    gate_ref,
    key_ref,
    value_ref,
    cot_ref,
    skip_ref,
    gain_ref,
    rate_wide_ref,
    res_wide_ref,
    rate_row_ref,
    res_row_ref,
    rate_chan_ref,
    mixer_ref,
    gq_ref,
    gk_ref,
    gv_ref,
    filt_ref,
    mixed_s,
    weight_s,
    back_s,
    sub_s,
    state_s,
    late_s,
    mask_tok,
    mask_mode,
    acc_s,
    total_s,
    own_s,
    in_s,
    out_s,
    got_s,
    own_b,
    in_b,
    out_b,
    got_b,
    norm_own,
    norm_got,
    part_s,
    part_got,
    send_sem,
    recv_sem,
    tp_send,
    tp_recv,
):
    here = lax.axis_index("ctx")
    side = lax.axis_index("tp")
    length, channels = gate_ref.shape
    subs = length // SUB
    blocks = channels // LANES
    in_block = LANES // members
    wide = in_block * SUB
    piece_rows = blocks * modes // ctx_count

    barrier = pltpu.get_barrier_semaphore()
    for d in range(1, ctx_count):
        pl.semaphore_signal(
            barrier, inc=1, device_id={"ctx": lax.rem(here + d, ctx_count)}, device_id_type=MESH
        )
    for d in range(1, tp_count):
        pl.semaphore_signal(
            barrier, inc=1, device_id={"tp": lax.rem(side + d, tp_count)}, device_id_type=MESH
        )

    mask_tok[...] = (
        iota((wide, LANES), 0) // SUB == iota((wide, LANES), 1) // members
    ).astype(F32).astype(BF16)
    mask_mode[...] = (
        iota((in_block * modes, LANES), 0) // modes == iota((in_block * modes, LANES), 1) // members
    ).astype(F32).astype(BF16)
    acc_s[...] = jnp.zeros_like(acc_s)
    total_s[...] = jnp.zeros_like(total_s)

    def lanes(j, width=LANES):
        return pl.ds(pl.multiple_of(j * width, width), width)

    def stack(value, mask):
        copies = mask.shape[0] // value.shape[0]
        return jnp.concatenate([value] * copies, axis=0) * mask

    def tokens_stack(value):
        mask = mask_tok[...]
        return jnp.concatenate(
            [stack(value[n * SUB : (n + 1) * SUB], mask) for n in range(subs)], axis=1
        )

    def carry_product(table, states):
        mask = mask_mode[...]
        split = [halves(s) for s in states]
        right = [
            jnp.concatenate([stack(s[k], mask) for s in split], axis=1) for k in range(2)
        ]
        return product(halves(table), right)

    def put_state(ref, j, value):
        if piece_rows >= modes:
            per = piece_rows // modes
            ref[j // per, pl.ds(pl.multiple_of((j % per) * modes, modes), modes)] = value
        else:
            per = modes // piece_rows
            for q in range(per):
                ref[j * per + q] = value[q * piece_rows : (q + 1) * piece_rows]

    def take_state(ref, j):
        if piece_rows >= modes:
            per = piece_rows // modes
            return ref[j // per, pl.ds(pl.multiple_of((j % per) * modes, modes), modes)]
        per = modes // piece_rows
        return jnp.concatenate([ref[j * per + q] for q in range(per)], axis=0)

    def chan_rate(j):
        return rate_chan_ref[pl.ds(pl.multiple_of(j * modes, modes), modes)]

    def signal_of(j):
        at = lanes(j)
        return key_ref[:, at].astype(F32) * value_ref[:, at].astype(F32)

    def strided(row, first):
        parts = []
        for h in range(wide // LANES):
            part = jnp.broadcast_to(row[:, h * LANES : (h + 1) * LANES], (SUB, LANES))
            parts.append(pltpu.roll(part, first, 1, stride=1, stride_axis=0))
        return jnp.concatenate(parts, axis=1)

    row_id = iota((SUB, wide), 0)
    lane_id = iota((SUB, wide), 1) % SUB
    offset = (iota((modes, wide), 1) % SUB).astype(F32)

    def first_pass(j, _):
        at = lanes(j)
        rate = rate_wide_ref[:, lanes(j, wide)]
        res = res_wide_ref[:, lanes(j, wide)]
        ending = jnp.exp(-rate * (SUB - offset))
        taps = jnp.sum(res * jnp.exp(-rate * (SUB - 1.0 - offset)), axis=0, keepdims=True)
        toeplitz = jnp.where(lane_id <= row_id, strided(taps, LANES - SUB + 1), 0.0)
        table = jnp.concatenate([toeplitz, ending, ending * (SUB - offset)], axis=0)
        high, low = halves(signal_of(j))
        out = product(halves(table), (tokens_stack(high), tokens_stack(low)))
        for n in range(subs):
            mixed_s[n * SUB : (n + 1) * SUB, at] = out[:SUB, n * LANES : (n + 1) * LANES]
        sub_s[j] = out[SUB:]
        step = jnp.exp(-chan_rate(j) * SUB)
        state = out[SUB : SUB + modes, :LANES]
        for n in range(1, subs):
            state = step * state + out[SUB : SUB + modes, n * LANES : (n + 1) * LANES]
        put_state(own_s, j, state)
        return 0

    lax.fori_loop(0, blocks, first_pass, 0)
    pl.semaphore_wait(barrier, ctx_count - 1 + tp_count - 1)

    def spread(source, target, phase, by_target):
        copies = []
        for d in range(1, ctx_count):
            there = lax.rem(here + d, ctx_count)
            copy = pltpu.make_async_remote_copy(
                src_ref=source.at[there] if by_target else source,
                dst_ref=target.at[here],
                send_sem=send_sem.at[phase, d],
                recv_sem=recv_sem.at[phase, d],
                device_id={"ctx": there},
                device_id_type=MESH,
            )
            copy.start()
            copies.append(copy)
        target[here] = source[here] if by_target else source[...]
        for copy in copies:
            copy.wait()

    def owned_decay():
        if piece_rows >= modes:
            per = piece_rows // modes
            return jnp.exp(
                -length * rate_chan_ref[pl.ds(pl.multiple_of(here * piece_rows, piece_rows), piece_rows)]
            )
        per = modes // piece_rows
        whole = rate_chan_ref[pl.ds(pl.multiple_of(here // per * modes, modes), modes)]
        rates = whole[:piece_rows]
        for q in range(1, per):
            rates = jnp.where(
                here % per == q, whole[q * piece_rows : (q + 1) * piece_rows], rates
            )
        return jnp.exp(-length * rates)

    def join(source, target, reverse):
        decay = owned_decay()

        def step(k, state):
            at = ctx_count - 1 - k if reverse else k
            target[at] = state
            return decay * state + source[at]

        lax.fori_loop(0, ctx_count, step, jnp.zeros((piece_rows, LANES), F32), unroll=True)

    spread(own_s, in_s, 0, True)
    join(in_s, out_s, False)
    spread(out_s, got_s, 1, True)

    time = (iota((SUB, in_block * modes), 0)).astype(F32)

    def second_pass(j, _):
        at = lanes(j)
        step = jnp.exp(-chan_rate(j) * SUB)
        state, moment = take_state(got_s, j), jnp.zeros((modes, LANES), F32)
        states = []
        for n in range(subs):
            states.append(state)
            state_s[j, n] = jnp.concatenate([state, moment], axis=0)
            part = sub_s[j, :, n * LANES : (n + 1) * LANES]
            moment = step * (moment + SUB * state) + part[modes:]
            state = step * state + part[:modes]
        late_s[j] = moment
        rate = rate_row_ref[pl.ds(j, 1)]
        table = res_row_ref[pl.ds(j, 1)] * jnp.exp(-rate * time)
        carried = carry_product(table, states)
        carried = jnp.concatenate(
            [carried[:, n * LANES : (n + 1) * LANES] for n in range(subs)], axis=0
        )
        mixed = mixed_s[:, at] + carried + skip_ref[:, at] * signal_of(j)
        mixed_s[:, at] = mixed
        premix = gate_ref[:, at].astype(F32) * mixed
        pull = cot_ref[:, at].astype(F32) * gain_ref[:, at]
        acc_s[0] += premix * premix
        acc_s[1] += pull * premix
        return 0

    lax.fori_loop(0, blocks, second_pass, 0)

    for k in range(2):
        row = jnp.sum(acc_s[k].T, axis=0, keepdims=True)
        norm_own[4 * k : 4 * k + 4] = jnp.broadcast_to(row, (4, length))
    copies = []
    for d in range(1, tp_count):
        copy = pltpu.make_async_remote_copy(
            src_ref=norm_own,
            dst_ref=norm_got.at[side],
            send_sem=tp_send.at[d],
            recv_sem=tp_recv.at[d],
            device_id={"tp": lax.rem(side + d, tp_count)},
            device_id_type=MESH,
        )
        copy.start()
        copies.append(copy)
    norm_got[side] = norm_own[...]
    for copy in copies:
        copy.wait()
    sums = norm_got[0]
    for k in range(1, tp_count):
        sums = sums + norm_got[k]
    square_row = lax.rsqrt(sums[0:1] / full_width + EPSILON)
    inner_row = sums[4:5] * square_row / full_width
    acc_s[0] = jnp.broadcast_to(square_row, (LANES, length)).T
    acc_s[1] = jnp.broadcast_to(inner_row, (LANES, length)).T

    group_of_lane = iota((LANES, LANES), 0) // members
    group_of_wide = iota((wide, LANES), 0) // SUB
    lane_of = iota((LANES, LANES), 1)
    lane_of_wide = iota((wide, LANES), 1)
    half_row = iota((SUB, LANES), 0)

    def third_pass(j, _):
        at = lanes(j)
        inverse, inner = acc_s[0], acc_s[1]
        mixed = mixed_s[:, at]
        gate = gate_ref[:, at].astype(F32)
        gain = gain_ref[:, at]
        normed = gate * mixed * inverse
        mixer_ref[:, at] = (normed * gain).astype(BF16)
        dpre = (cot_ref[:, at].astype(F32) * gain - normed * inner) * inverse
        gq_ref[:, at] = (dpre * mixed).astype(BF16)
        weight = dpre * gate
        weight_s[:, at] = weight
        rate = rate_wide_ref[:, lanes(j, wide)]
        res = res_wide_ref[:, lanes(j, wide)]
        start = jnp.exp(-rate * offset)
        taps = jnp.sum(res * start, axis=0, keepdims=True)
        toeplitz = jnp.where(lane_id >= row_id, strided(taps, 0), 0.0)
        table = jnp.concatenate([toeplitz, start, start * offset], axis=0)
        high, low = halves(weight)
        right = (tokens_stack(high), tokens_stack(low))
        out = product(halves(table), right)
        for n in range(subs):
            back_s[n * SUB : (n + 1) * SUB, at] = out[:SUB, n * LANES : (n + 1) * LANES]
        sub_s[j] = out[SUB:]
        step = jnp.exp(-chan_rate(j) * SUB)
        last = (subs - 1) * LANES
        state = out[SUB : SUB + modes, last:]
        for n in range(subs - 2, -1, -1):
            state = step * state + out[SUB : SUB + modes, n * LANES : (n + 1) * LANES]
        put_state(own_b, j, state)

        signal = signal_of(j)
        left = tuple(
            jnp.concatenate([part[n * SUB : (n + 1) * SUB] for n in range(subs)], axis=1)
            for part in halves(signal)
        )
        pairs = jnp.where(lane_id >= row_id, product(left, right, dot_t), 0.0)
        lagged = []
        for h in range(wide // LANES):
            part = pairs[:, h * LANES : (h + 1) * LANES]
            bit = 1
            while bit < SUB:
                moved = pltpu.roll(part, LANES - bit, 1)
                part = jnp.where((half_row // bit) % 2 == 1, moved, part)
                bit *= 2
            lagged.append(jnp.sum(part, axis=0, keepdims=True))
        lagged = jnp.concatenate(lagged, axis=1)
        zeroth = start * lagged
        local = jnp.concatenate([zeroth, zeroth * offset], axis=0)
        to_group = (group_of_wide + j * in_block == lane_of_wide).astype(F32).astype(BF16)
        total = exact_dot(local, to_group)

        cross = jnp.zeros((modes, LANES), F32)
        cross_moment = jnp.zeros((modes, LANES), F32)
        for n in range(subs):
            part = out[SUB:, n * LANES : (n + 1) * LANES]
            both = state_s[j, n]
            cross += part[:modes] * both[:modes]
            cross_moment += part[modes:] * both[:modes] + part[:modes] * both[modes:]
        to_group = (group_of_lane + j * in_block == lane_of).astype(F32).astype(BF16)
        total += exact_dot(jnp.concatenate([cross, cross_moment], axis=0), to_group)
        total_s[...] += total
        return 0

    lax.fori_loop(0, blocks, third_pass, 0)

    spread(own_b, in_b, 2, True)
    join(in_b, out_b, True)
    spread(out_b, got_b, 3, True)

    def fourth_pass(j, _):
        at = lanes(j)
        step = jnp.exp(-chan_rate(j) * SUB)
        state = take_state(got_b, j)
        to_group = (group_of_lane + j * in_block == lane_of).astype(F32).astype(BF16)
        total_s[modes:] += exact_dot(state * late_s[j], to_group)
        states = []
        for n in range(subs - 1, -1, -1):
            states.append(state)
            state = step * state + sub_s[j, :modes, n * LANES : (n + 1) * LANES]
        states.reverse()
        rate = rate_row_ref[pl.ds(j, 1)]
        table = res_row_ref[pl.ds(j, 1)] * jnp.exp(-rate * (SUB - time))
        carried = carry_product(table, states)
        carried = jnp.concatenate(
            [carried[:, n * LANES : (n + 1) * LANES] for n in range(subs)], axis=0
        )
        grad = back_s[:, at] + carried + skip_ref[:, at] * weight_s[:, at]
        gk_ref[:, at] = (grad * value_ref[:, at].astype(F32)).astype(BF16)
        gv_ref[:, at] = (grad * key_ref[:, at].astype(F32)).astype(BF16)
        return 0

    lax.fori_loop(0, blocks, fourth_pass, 0)

    part_s[...] = total_s[...]
    spread(part_s, part_got, 4, False)
    sums = part_got[0]
    for k in range(1, ctx_count):
        sums = sums + part_got[k]
    filt_ref[...] = sums


def per_device(out_gate, key_proj, value_proj, residue, log_decay, skip, gain, cotangent):
    length, channels = out_gate.shape
    groups, modes = residue.shape
    members = channels // groups
    ctx_count, tp_count = lax.axis_size("ctx"), lax.axis_size("tp")
    blocks = channels // LANES
    in_block = LANES // members
    subs = length // SUB
    wide = in_block * SUB
    piece_rows = blocks * modes // ctx_count
    rate = jnp.exp(log_decay)
    rate_wide = jnp.repeat(rate.T, SUB, axis=1)
    res_wide = jnp.repeat(residue.T, SUB, axis=1)
    rate_row = rate.reshape(blocks, in_block * modes)
    res_row = residue.reshape(blocks, in_block * modes)
    rate_chan = (
        jnp.repeat(rate.T, members, axis=1)
        .reshape(modes, blocks, LANES)
        .transpose(1, 0, 2)
        .reshape(blocks * modes, LANES)
    )
    pieces = pltpu.VMEM((ctx_count, piece_rows, LANES), F32)
    wide_out = jax.ShapeDtypeStruct((length, channels), BF16)
    vmem = pl.BlockSpec(memory_space=pltpu.VMEM)
    mixer_out, grad_q, grad_k, grad_v, filt = pl.pallas_call(
        functools.partial(
            kernel, ctx_count, tp_count, float(channels * tp_count), modes, members
        ),
        out_shape=[wide_out] * 4 + [jax.ShapeDtypeStruct((2 * modes, groups), F32)],
        in_specs=[vmem] * 11,
        out_specs=[vmem] * 5,
        scratch_shapes=[
            pltpu.VMEM((length, channels), F32),
            pltpu.VMEM((length, channels), F32),
            pltpu.VMEM((length, channels), F32),
            pltpu.VMEM((blocks, 2 * modes, subs * LANES), F32),
            pltpu.VMEM((blocks, subs, 2 * modes, LANES), F32),
            pltpu.VMEM((blocks, modes, LANES), F32),
            pltpu.VMEM((wide, LANES), BF16),
            pltpu.VMEM((in_block * modes, LANES), BF16),
            pltpu.VMEM((2, length, LANES), F32),
            pltpu.VMEM((2 * modes, groups), F32),
            pieces, pieces, pieces, pieces,
            pieces, pieces, pieces, pieces,
            pltpu.VMEM((8, length), F32),
            pltpu.VMEM((tp_count, 8, length), F32),
            pltpu.VMEM((2 * modes, groups), F32),
            pltpu.VMEM((ctx_count, 2 * modes, groups), F32),
            pltpu.SemaphoreType.DMA((5, ctx_count)),
            pltpu.SemaphoreType.DMA((5, ctx_count)),
            pltpu.SemaphoreType.DMA((tp_count,)),
            pltpu.SemaphoreType.DMA((tp_count,)),
        ],
        compiler_params=pltpu.CompilerParams(
            collective_id=0, has_side_effects=True, vmem_limit_bytes=48 * 1024 * 1024
        ),
        name="mixer",
    )(
        out_gate, key_proj, value_proj, cotangent, skip[None], gain[None],
        rate_wide, res_wide, rate_row, res_row, rate_chan,
    )
    token_total = length * ctx_count
    grad_residue = filt[:modes].T / token_total
    grad_log_decay = -residue * rate * filt[modes:].T / token_total
    return mixer_out, grad_q, grad_k, grad_v, grad_residue, grad_log_decay


def solution(mesh):
    wide, table, row = P("ctx", "tp"), P("tp", None), P("tp")
    return jax.shard_map(
        per_device,
        mesh=mesh,
        in_specs=(wide, wide, wide, table, table, row, row, wide),
        out_specs=(wide, wide, wide, wide, table, table),
        check_vma=False,
    )
```

```python
import functools

import jax
import jax.numpy as jnp
from jax import lax
from jax.experimental import pallas as pl
from jax.experimental.pallas import tpu as pltpu
from jax.sharding import PartitionSpec as P

EPSILON = 1e-06
LANES = 128
SUB = 32
F32 = jnp.float32
BF16 = jnp.bfloat16
MESH = pl.DeviceIdType.MESH


def halves(value):
    high = value.astype(BF16)
    return high, (value - high.astype(F32)).astype(BF16)


def dot(a, b):
    return jnp.dot(a, b, preferred_element_type=F32)


def dot_t(a, b):
    return lax.dot_general(a, b, (((1,), (1,)), ((), ())), preferred_element_type=F32)


def product(left, right, multiply=dot):
    rows = left[0].shape[0]
    both = multiply(jnp.concatenate(left, axis=0), right[0])
    return both[:rows] + both[rows:] + multiply(left[0], right[1])


def exact_dot(value, ones):
    rows = value.shape[0]
    high, rest = value.astype(BF16), None
    rest = value - high.astype(F32)
    mid = rest.astype(BF16)
    low = (rest - mid.astype(F32)).astype(BF16)
    out = dot(jnp.concatenate([high, mid, low], axis=0), ones)
    return out[:rows] + out[rows : 2 * rows] + out[2 * rows :]


def iota(shape, dim):
    return lax.broadcasted_iota(jnp.int32, shape, dim)


def transposed(value, eye):
    high = value.astype(BF16)
    rest = value - high.astype(F32)
    mid = rest.astype(BF16)
    low = (rest - mid.astype(F32)).astype(BF16)
    return dot_t(eye, high) + dot_t(eye, mid) + dot_t(eye, low)


def unit(size):
    return (iota((size, size), 0) == iota((size, size), 1)).astype(F32).astype(BF16)


def kernel(
    ctx_count,
    tp_count,
    full_width,
    gate_ref,
    key_ref,
    value_ref,
    cot_ref,
    skip_ref,
    gain_ref,
    res_ref,
    log_ref,
    mixer_ref,
    gq_ref,
    gk_ref,
    gv_ref,
    filt_ref,
    mixed_s,
    weight_s,
    back_s,
    sub_s,
    state_s,
    late_s,
    mask_tok,
    mask_mode,
    widen,
    wide_s,
    row_s,
    acc_s,
    total_s,
    own_s,
    in_s,
    out_s,
    got_s,
    own_b,
    in_b,
    out_b,
    got_b,
    norm_own,
    norm_got,
    part_s,
    part_got,
    send_sem,
    recv_sem,
    tp_send,
    tp_recv,
):
    here = lax.axis_index("ctx")
    side = lax.axis_index("tp")
    length, channels = gate_ref.shape
    modes, groups = res_ref.shape
    members = channels // groups
    subs = length // SUB
    blocks = channels // LANES
    in_block = LANES // members
    wide = in_block * SUB
    piece_rows = blocks * modes // ctx_count
    per = piece_rows // modes

    barrier = pltpu.get_barrier_semaphore()
    for d in range(1, ctx_count):
        pl.semaphore_signal(
            barrier, inc=1, device_id={"ctx": lax.rem(here + d, ctx_count)}, device_id_type=MESH
        )
    for d in range(1, tp_count):
        pl.semaphore_signal(
            barrier, inc=1, device_id={"tp": lax.rem(side + d, tp_count)}, device_id_type=MESH
        )

    mask_tok[...] = (
        iota((wide, LANES), 0) // SUB == iota((wide, LANES), 1) // members
    ).astype(F32).astype(BF16)
    mask_mode[...] = (
        iota((in_block * modes, LANES), 0) // modes == iota((in_block * modes, LANES), 1) // members
    ).astype(F32).astype(BF16)
    widen[:, :wide] = (iota((groups, wide), 0) == iota((groups, wide), 1) // SUB).astype(F32).astype(BF16)
    widen[:, wide:] = (
        iota((groups, LANES), 0) == iota((groups, LANES), 1) // members
    ).astype(F32).astype(BF16)
    acc_s[...] = jnp.zeros_like(acc_s)
    total_s[...] = jnp.zeros_like(total_s)

    def lanes(j, width=LANES):
        return pl.ds(pl.multiple_of(j * width, width), width)

    def stack(value, mask):
        copies = mask.shape[0] // value.shape[0]
        return jnp.concatenate([value] * copies, axis=0) * mask

    def tokens_stack(value):
        mask = mask_tok[...]
        return jnp.concatenate(
            [stack(value[n * SUB : (n + 1) * SUB], mask) for n in range(subs)], axis=1
        )

    def carry_product(table, states):
        mask = mask_mode[...]
        split = [halves(s) for s in states]
        right = [
            jnp.concatenate([stack(s[k], mask) for s in split], axis=1) for k in range(2)
        ]
        out = product(halves(table), right)
        return jnp.concatenate(
            [out[:, n * LANES : (n + 1) * LANES] for n in range(subs)], axis=0
        )

    def put_state(ref, j, value):
        if per:
            ref[j // per, pl.ds(pl.multiple_of((j % per) * modes, modes), modes)] = value
        else:
            count = modes // piece_rows
            for q in range(count):
                ref[j * count + q] = value[q * piece_rows : (q + 1) * piece_rows]

    def take_state(ref, j):
        if per:
            return ref[j // per, pl.ds(pl.multiple_of((j % per) * modes, modes), modes)]
        count = modes // piece_rows
        return jnp.concatenate([ref[j * count + q] for q in range(count)], axis=0)

    def rate_wide(j):
        return wide_s[j, :modes, :wide]

    def res_wide(j):
        return wide_s[j, modes:, :wide]

    def chan_rate(j):
        return wide_s[j, :modes, wide:]

    def signal_of(j):
        at = lanes(j)
        return key_ref[:, at].astype(F32) * value_ref[:, at].astype(F32)

    def strided(row, first):
        parts = []
        for h in range(wide // LANES):
            part = jnp.broadcast_to(row[:, h * LANES : (h + 1) * LANES], (SUB, LANES))
            parts.append(pltpu.roll(part, first, 1, stride=1, stride_axis=0))
        return jnp.concatenate(parts, axis=1)

    def batch(compute, store, js):
        results = [compute(j) for j in js]
        for j, result in zip(js, results):
            store(j, *result)

    def batches(compute, store, first, last, size):
        def step(i, _):
            batch(compute, store, [first + i * size + b for b in range(size)])
            return 0

        lax.fori_loop(0, (last - first) // size, step, 0)

    def transfer(source, target, phase, d, by_target=True):
        there = lax.rem(here + d, ctx_count)
        return pltpu.make_async_remote_copy(
            src_ref=source.at[there] if by_target else source,
            dst_ref=target.at[here],
            send_sem=send_sem.at[phase, d],
            recv_sem=recv_sem.at[phase, d],
            device_id={"ctx": there},
            device_id_type=MESH,
        )

    def all_others(act):
        def step(d, _):
            act(d)
            return 0

        lax.fori_loop(1, ctx_count, step, 0)

    def blocks_then_send(compute, store, source, target, phase):
        if per:
            def step(d, _):
                piece = lax.rem(here + d, ctx_count)
                batch(compute, store, [piece * per + b for b in range(per)])
                transfer(source, target, phase, d).start()
                return 0

            lax.fori_loop(1, ctx_count, step, 0)
            batch(compute, store, [here * per + b for b in range(per)])
        else:
            batches(compute, store, 0, blocks, 2)
            all_others(lambda d: transfer(source, target, phase, d).start())
        target[here] = source[here]

    def receive_then_blocks(compute, store, source, target, phase):
        target[here] = source[here]
        if per:
            batch(compute, store, [here * per + b for b in range(per)])

            def step(d, _):
                transfer(source, target, phase, d).wait_recv()
                piece = lax.rem(here - d + ctx_count, ctx_count)
                batch(compute, store, [piece * per + b for b in range(per)])
                return 0

            lax.fori_loop(1, ctx_count, step, 0)
        else:
            all_others(lambda d: transfer(source, target, phase, d).wait_recv())
            batches(compute, store, 0, blocks, 2)

    def owned_decay():
        if per:
            rates = jnp.concatenate([chan_rate(here * per + b) for b in range(per)], axis=0)
            return jnp.exp(-length * rates)
        count = modes // piece_rows
        whole = chan_rate(here // count)
        rates = whole[:piece_rows]
        for q in range(1, count):
            rates = jnp.where(
                here % count == q, whole[q * piece_rows : (q + 1) * piece_rows], rates
            )
        return jnp.exp(-length * rates)

    def join(own, source, target, result, phase, reverse):
        decay = owned_decay()
        all_others(lambda d: transfer(own, source, phase, d).wait_recv())

        def step(k, state):
            at = ctx_count - 1 - k if reverse else k
            target[at] = state
            return decay * state + source[at]

        lax.fori_loop(0, ctx_count, step, jnp.zeros((piece_rows, LANES), F32), unroll=True)
        all_others(lambda d: transfer(target, result, phase + 1, d).start())

    eye = unit(groups)
    tables = jnp.concatenate([jnp.exp(log_ref[...]), res_ref[...]], axis=0)
    rates, residues = transposed(tables[:modes], eye), transposed(tables[modes:], eye)
    spread_modes = (
        iota((modes, LANES), 0) == iota((modes, LANES), 1) % modes
    ).astype(F32).astype(BF16)
    own_row = iota((in_block, LANES), 0) == iota((in_block, LANES), 1) // modes
    widener = widen[...]
    for j in range(blocks):
        rolled = pltpu.roll(tables, (groups - j * in_block) % groups, 1)
        wide_s[j] = exact_dot(rolled, widener)
        rows = slice(j * in_block, (j + 1) * in_block)
        flat = exact_dot(jnp.concatenate([rates[rows], residues[rows]], axis=0), spread_modes)
        for q in range(2):
            part = jnp.where(own_row, flat[q * in_block : (q + 1) * in_block], 0.0)
            row_s[q, j : j + 1] = jnp.sum(part, axis=0, keepdims=True)

    row_id = iota((SUB, wide), 0)
    lane_id = iota((SUB, wide), 1) % SUB
    offset = (iota((modes, wide), 1) % SUB).astype(F32)
    time = iota((SUB, in_block * modes), 0).astype(F32)

    def states_of(j):
        ending = jnp.exp(-rate_wide(j) * (SUB - offset))
        table = jnp.concatenate([ending, ending * (SUB - offset)], axis=0)
        high, low = halves(signal_of(j))
        out = product(halves(table), (tokens_stack(high), tokens_stack(low)))
        step = jnp.exp(-chan_rate(j) * SUB)
        state = out[:modes, :LANES]
        for n in range(1, subs):
            state = step * state + out[:modes, n * LANES : (n + 1) * LANES]
        return out, state

    def states_put(j, out, state):
        sub_s[j] = out
        put_state(own_s, j, state)

    def local_of(j):
        taps = jnp.sum(
            res_wide(j) * jnp.exp(-rate_wide(j) * (SUB - 1.0 - offset)), axis=0, keepdims=True
        )
        toeplitz = jnp.where(lane_id <= row_id, strided(taps, LANES - SUB + 1), 0.0)
        signal = signal_of(j)
        high, low = halves(signal)
        out = product(halves(toeplitz), (tokens_stack(high), tokens_stack(low)))
        out = jnp.concatenate([out[:, n * LANES : (n + 1) * LANES] for n in range(subs)], axis=0)
        return (out + skip_ref[:, lanes(j)] * signal,)

    def local_put(j, out):
        mixed_s[:, lanes(j)] = out

    def carried_of(j):
        at = lanes(j)
        step = jnp.exp(-chan_rate(j) * SUB)
        state, moment = take_state(got_s, j), jnp.zeros((modes, LANES), F32)
        states, saved = [], []
        for n in range(subs):
            states.append(state)
            saved.append(jnp.concatenate([state, moment], axis=0))
            part = sub_s[j, :, n * LANES : (n + 1) * LANES]
            moment = step * (moment + SUB * state) + part[modes:]
            state = step * state + part[:modes]
        table = row_s[1, pl.ds(j, 1)] * jnp.exp(-row_s[0, pl.ds(j, 1)] * time)
        mixed = mixed_s[:, at] + carry_product(table, states)
        premix = gate_ref[:, at].astype(F32) * mixed
        pull = cot_ref[:, at].astype(F32) * gain_ref[:, at]
        return saved, moment, mixed, premix * premix, pull * premix

    def carried_put(j, saved, moment, mixed, square, inner):
        for n in range(subs):
            state_s[j, n] = saved[n]
        late_s[j] = moment
        mixed_s[:, lanes(j)] = mixed
        acc_s[0] += square
        acc_s[1] += inner

    pl.semaphore_wait(barrier, ctx_count - 1 + tp_count - 1)
    half = blocks // 2
    blocks_then_send(states_of, states_put, own_s, in_s, 0)
    batches(local_of, local_put, 0, half, 4)
    join(own_s, in_s, out_s, got_s, 0, False)
    batches(local_of, local_put, half, blocks, 4)
    receive_then_blocks(carried_of, carried_put, out_s, got_s, 1)

    for k in range(2):
        row = jnp.sum(acc_s[k].T, axis=0, keepdims=True)
        norm_own[4 * k : 4 * k + 4] = jnp.broadcast_to(row, (4, length))
    copies = []
    for d in range(1, tp_count):
        copy = pltpu.make_async_remote_copy(
            src_ref=norm_own,
            dst_ref=norm_got.at[side],
            send_sem=tp_send.at[d],
            recv_sem=tp_recv.at[d],
            device_id={"tp": lax.rem(side + d, tp_count)},
            device_id_type=MESH,
        )
        copy.start()
        copies.append(copy)
    norm_got[side] = norm_own[...]
    for copy in copies:
        copy.wait()
    sums = norm_got[0]
    for k in range(1, tp_count):
        sums = sums + norm_got[k]
    inverse_row = lax.rsqrt(sums[0:1] / full_width + EPSILON)
    inner_row = sums[4:5] * inverse_row / full_width
    acc_s[0] = jnp.broadcast_to(inverse_row, (LANES, length)).T
    acc_s[1] = jnp.broadcast_to(inner_row, (LANES, length)).T

    group_of_lane = iota((LANES, LANES), 0) // members
    group_of_wide = iota((wide, LANES), 0) // SUB
    lane_of = iota((LANES, LANES), 1)
    lane_of_wide = iota((wide, LANES), 1)
    half_row = iota((SUB, LANES), 0)

    def weight_of(j):
        at = lanes(j)
        inverse, inner = acc_s[0], acc_s[1]
        gate = gate_ref[:, at].astype(F32)
        normed = gate * mixed_s[:, at] * inverse
        dpre = (cot_ref[:, at].astype(F32) * gain_ref[:, at] - normed * inner) * inverse
        weight = dpre * gate
        start = jnp.exp(-rate_wide(j) * offset)
        table = jnp.concatenate([start, start * offset], axis=0)
        high, low = halves(weight)
        out = product(halves(table), (tokens_stack(high), tokens_stack(low)))
        step = jnp.exp(-chan_rate(j) * SUB)
        state = out[:modes, (subs - 1) * LANES :]
        for n in range(subs - 2, -1, -1):
            state = step * state + out[:modes, n * LANES : (n + 1) * LANES]
        return weight, out, state

    def weight_put(j, weight, out, state):
        weight_s[:, lanes(j)] = weight
        sub_s[j] = out
        put_state(own_b, j, state)

    def inside_of(j):
        at = lanes(j)
        inverse, inner = acc_s[0], acc_s[1]
        mixed = mixed_s[:, at]
        gain = gain_ref[:, at]
        normed = gate_ref[:, at].astype(F32) * mixed * inverse
        dpre = (cot_ref[:, at].astype(F32) * gain - normed * inner) * inverse
        weight = weight_s[:, at]
        start = jnp.exp(-rate_wide(j) * offset)
        taps = jnp.sum(res_wide(j) * start, axis=0, keepdims=True)
        toeplitz = jnp.where(lane_id >= row_id, strided(taps, 0), 0.0)
        high, low = halves(weight)
        right = (tokens_stack(high), tokens_stack(low))
        back = product(halves(toeplitz), right)
        back = jnp.concatenate([back[:, n * LANES : (n + 1) * LANES] for n in range(subs)], axis=0)

        left = tuple(
            jnp.concatenate([part[n * SUB : (n + 1) * SUB] for n in range(subs)], axis=1)
            for part in halves(signal_of(j))
        )
        pairs = jnp.where(lane_id >= row_id, product(left, right, dot_t), 0.0)
        lagged = []
        for h in range(wide // LANES):
            part = pairs[:, h * LANES : (h + 1) * LANES]
            bit = 1
            while bit < SUB:
                moved = pltpu.roll(part, LANES - bit, 1)
                part = jnp.where((half_row // bit) % 2 == 1, moved, part)
                bit *= 2
            lagged.append(jnp.sum(part, axis=0, keepdims=True))
        zeroth = start * jnp.concatenate(lagged, axis=1)
        local = jnp.concatenate([zeroth, zeroth * offset], axis=0)
        to_group = (group_of_wide + j * in_block == lane_of_wide).astype(F32).astype(BF16)
        total = exact_dot(local, to_group)

        cross = jnp.zeros((modes, LANES), F32)
        cross_moment = jnp.zeros((modes, LANES), F32)
        for n in range(subs):
            part = sub_s[j, :, n * LANES : (n + 1) * LANES]
            both = state_s[j, n]
            cross += part[:modes] * both[:modes]
            cross_moment += part[modes:] * both[:modes] + part[:modes] * both[modes:]
        to_group = (group_of_lane + j * in_block == lane_of).astype(F32).astype(BF16)
        total += exact_dot(jnp.concatenate([cross, cross_moment], axis=0), to_group)
        return (
            (normed * gain).astype(BF16),
            (dpre * mixed).astype(BF16),
            back + skip_ref[:, at] * weight,
            total,
        )

    def inside_put(j, mixer, grad_q, back, total):
        at = lanes(j)
        mixer_ref[:, at] = mixer
        gq_ref[:, at] = grad_q
        back_s[:, at] = back
        total_s[...] += total

    def ending_of(j):
        to_group = (group_of_lane + j * in_block == lane_of).astype(F32).astype(BF16)
        return (exact_dot(take_state(got_b, j) * late_s[j], to_group),)

    def ending_put(j, total):
        total_s[modes:] += total

    def signal_grad_of(j):
        at = lanes(j)
        step = jnp.exp(-chan_rate(j) * SUB)
        state = take_state(got_b, j)
        states = []
        for n in range(subs - 1, -1, -1):
            states.append(state)
            state = step * state + sub_s[j, :modes, n * LANES : (n + 1) * LANES]
        states.reverse()
        table = row_s[1, pl.ds(j, 1)] * jnp.exp(-row_s[0, pl.ds(j, 1)] * (SUB - time))
        grad = back_s[:, at] + carry_product(table, states)
        return (
            (grad * value_ref[:, at].astype(F32)).astype(BF16),
            (grad * key_ref[:, at].astype(F32)).astype(BF16),
        )

    def signal_grad_put(j, grad_k, grad_v):
        gk_ref[:, lanes(j)] = grad_k
        gv_ref[:, lanes(j)] = grad_v

    blocks_then_send(weight_of, weight_put, own_b, in_b, 2)
    batches(inside_of, inside_put, 0, half, 2)
    join(own_b, in_b, out_b, got_b, 2, True)
    batches(inside_of, inside_put, half, blocks, 2)
    receive_then_blocks(ending_of, ending_put, out_b, got_b, 3)

    part_s[...] = total_s[...]
    all_others(lambda d: transfer(part_s, part_got, 4, d, False).start())
    part_got[here] = part_s[...]
    batches(signal_grad_of, signal_grad_put, 0, blocks, 4)
    all_others(lambda d: transfer(part_s, part_got, 4, d, False).wait())
    sums = part_got[0]
    for k in range(1, ctx_count):
        sums = sums + part_got[k]
    filt_ref[...] = sums

    def drain(d):
        for phase, (source, target) in enumerate(
            ((own_s, in_s), (out_s, got_s), (own_b, in_b), (out_b, got_b))
        ):
            transfer(source, target, phase, d).wait_send()

    all_others(drain)


def finish(
    token_total, mixer_ref, gq_ref, gk_ref, gv_ref, filt_ref, res_ref, log_ref,
    mixer_out, gq_out, gk_out, gv_out, res_out, log_out, sems,
):
    pairs = ((mixer_ref, mixer_out), (gq_ref, gq_out), (gk_ref, gk_out), (gv_ref, gv_out))
    copies = [
        pltpu.make_async_copy(source, target, sems.at[k])
        for k, (source, target) in enumerate(pairs)
    ]
    for copy in copies:
        copy.start()
    modes = res_ref.shape[0]
    res_out[...] = filt_ref[:modes] / token_total
    log_out[...] = -res_ref[...] * jnp.exp(log_ref[...]) * filt_ref[modes:] / token_total
    for copy in copies:
        copy.wait()


def per_device(out_gate, key_proj, value_proj, residue, log_decay, skip, gain, cotangent):
    length, channels = out_gate.shape
    groups, modes = residue.shape
    members = channels // groups
    ctx_count, tp_count = lax.axis_size("ctx"), lax.axis_size("tp")
    blocks = channels // LANES
    in_block = LANES // members
    subs = length // SUB
    wide = in_block * SUB
    piece_rows = blocks * modes // ctx_count
    pieces = pltpu.VMEM((ctx_count, piece_rows, LANES), F32)
    wide_out = jax.ShapeDtypeStruct((length, channels), BF16)
    table_out = jax.ShapeDtypeStruct((modes, groups), F32)
    vmem = pl.BlockSpec(memory_space=pltpu.VMEM)
    anywhere = pl.BlockSpec(memory_space=pl.ANY)
    results = pl.pallas_call(
        functools.partial(kernel, ctx_count, tp_count, float(channels * tp_count)),
        out_shape=[wide_out] * 4 + [jax.ShapeDtypeStruct((2 * modes, groups), F32)],
        in_specs=[vmem] * 8,
        out_specs=[vmem] * 5,
        scratch_shapes=[
            pltpu.VMEM((length, channels), F32),
            pltpu.VMEM((length, channels), F32),
            pltpu.VMEM((length, channels), F32),
            pltpu.VMEM((blocks, 2 * modes, subs * LANES), F32),
            pltpu.VMEM((blocks, subs, 2 * modes, LANES), F32),
            pltpu.VMEM((blocks, modes, LANES), F32),
            pltpu.VMEM((wide, LANES), BF16),
            pltpu.VMEM((in_block * modes, LANES), BF16),
            pltpu.VMEM((groups, wide + LANES), BF16),
            pltpu.VMEM((blocks, 2 * modes, wide + LANES), F32),
            pltpu.VMEM((2, blocks, LANES), F32),
            pltpu.VMEM((2, length, LANES), F32),
            pltpu.VMEM((2 * modes, groups), F32),
            pieces, pieces, pieces, pieces,
            pieces, pieces, pieces, pieces,
            pltpu.VMEM((8, length), F32),
            pltpu.VMEM((tp_count, 8, length), F32),
            pltpu.VMEM((2 * modes, groups), F32),
            pltpu.VMEM((ctx_count, 2 * modes, groups), F32),
            pltpu.SemaphoreType.DMA((5, ctx_count)),
            pltpu.SemaphoreType.DMA((5, ctx_count)),
            pltpu.SemaphoreType.DMA((tp_count,)),
            pltpu.SemaphoreType.DMA((tp_count,)),
        ],
        compiler_params=pltpu.CompilerParams(
            collective_id=0, has_side_effects=True, vmem_limit_bytes=40 * 1024 * 1024
        ),
        name="mixer",
    )(out_gate, key_proj, value_proj, cotangent, skip[None], gain[None], residue.T, log_decay.T)
    *wide_results, grad_residue, grad_log_decay = pl.pallas_call(
        functools.partial(finish, float(length * ctx_count)),
        out_shape=[wide_out] * 4 + [table_out] * 2,
        in_specs=[vmem] * 7,
        out_specs=[anywhere] * 4 + [vmem] * 2,
        scratch_shapes=[pltpu.SemaphoreType.DMA((4,))],
        name="finish",
    )(*results, residue.T, log_decay.T)
    return *wide_results, grad_residue.T, grad_log_decay.T


def solution(mesh):
    wide, table, row = P("ctx", "tp"), P("tp", None), P("tp")
    return jax.shard_map(
        per_device,
        mesh=mesh,
        in_specs=(wide, wide, wide, table, table, row, row, wide),
        out_specs=(wide, wide, wide, wide, table, table),
        check_vma=False,
    )
```

```python
import functools

import jax
import jax.numpy as jnp
from jax import lax
from jax.experimental import pallas as pl
from jax.experimental.pallas import tpu as pltpu
from jax.sharding import PartitionSpec as P

EPSILON = 1e-06
LANES = 128
SUB = 32
F32 = jnp.float32
BF16 = jnp.bfloat16
MESH = pl.DeviceIdType.MESH


def halves(value):
    high = value.astype(BF16)
    return high, (value - high.astype(F32)).astype(BF16)


def dot(a, b):
    return jnp.dot(a, b, preferred_element_type=F32)


def dot_t(a, b):
    return lax.dot_general(a, b, (((1,), (1,)), ((), ())), preferred_element_type=F32)


def product(left, right, multiply=dot):
    rows = left[0].shape[0]
    both = multiply(jnp.concatenate(left, axis=0), right[0])
    return both[:rows] + both[rows:] + multiply(left[0], right[1])


def exact_dot(value, ones):
    rows = value.shape[0]
    high, rest = value.astype(BF16), None
    rest = value - high.astype(F32)
    mid = rest.astype(BF16)
    low = (rest - mid.astype(F32)).astype(BF16)
    out = dot(jnp.concatenate([high, mid, low], axis=0), ones)
    return out[:rows] + out[rows : 2 * rows] + out[2 * rows :]


def iota(shape, dim):
    return lax.broadcasted_iota(jnp.int32, shape, dim)


def transposed(value, eye):
    high = value.astype(BF16)
    rest = value - high.astype(F32)
    mid = rest.astype(BF16)
    low = (rest - mid.astype(F32)).astype(BF16)
    return dot_t(eye, high) + dot_t(eye, mid) + dot_t(eye, low)


def unit(size):
    return (iota((size, size), 0) == iota((size, size), 1)).astype(F32).astype(BF16)


def kernel(
    ctx_count,
    tp_count,
    full_width,
    gate_in,
    key_in,
    value_in,
    cot_in,
    skip_in,
    gain_in,
    res_in,
    log_in,
    mixer_out,
    gq_out,
    gk_out,
    gv_out,
    res_out,
    log_out,
    gate_ref,
    key_ref,
    value_ref,
    cot_ref,
    skip_ref,
    gain_ref,
    res_ref,
    log_ref,
    mixer_ref,
    gq_ref,
    gk_ref,
    gv_ref,
    filt_ref,
    mixed_s,
    weight_s,
    back_s,
    sub_s,
    state_s,
    late_s,
    mask_tok,
    mask_mode,
    widen,
    wide_s,
    table_s,
    toeplitz_s,
    local_s,
    cross_s,
    row_s,
    acc_s,
    own_s,
    in_s,
    out_s,
    got_s,
    own_b,
    in_b,
    out_b,
    got_b,
    norm_own,
    norm_got,
    part_s,
    part_got,
    send_sem,
    recv_sem,
    tp_send,
    tp_recv,
    load_sem,
    store_sem,
    part_sem,
):
    here = lax.axis_index("ctx")
    side = lax.axis_index("tp")
    length, channels = gate_ref.shape
    modes, groups = res_ref.shape
    members = channels // groups
    subs = length // SUB
    blocks = channels // LANES
    in_block = LANES // members
    wide = in_block * SUB
    piece_rows = blocks * modes // ctx_count
    per = piece_rows // modes

    loads = [
        pltpu.make_async_copy(source, target, load_sem.at[k])
        for k, (source, target) in enumerate(
            (
                (res_in, res_ref),
                (log_in, log_ref),
                (key_in, key_ref),
                (value_in, value_ref),
                (skip_in, skip_ref),
                (gate_in, gate_ref),
                (cot_in, cot_ref),
                (gain_in, gain_ref),
            )
        )
    ]
    for load in loads:
        load.start()

    barrier = pltpu.get_barrier_semaphore()
    for d in range(1, ctx_count):
        pl.semaphore_signal(
            barrier, inc=1, device_id={"ctx": lax.rem(here + d, ctx_count)}, device_id_type=MESH
        )
    for d in range(1, tp_count):
        pl.semaphore_signal(
            barrier, inc=1, device_id={"tp": lax.rem(side + d, tp_count)}, device_id_type=MESH
        )

    mask_tok[...] = (
        iota((wide, LANES), 0) // SUB == iota((wide, LANES), 1) // members
    ).astype(F32).astype(BF16)
    mask_mode[...] = (
        iota((in_block * modes, LANES), 0) // modes == iota((in_block * modes, LANES), 1) // members
    ).astype(F32).astype(BF16)
    widen[:, :wide] = (iota((groups, wide), 0) == iota((groups, wide), 1) // SUB).astype(F32).astype(BF16)
    widen[:, wide:] = (
        iota((groups, LANES), 0) == iota((groups, LANES), 1) // members
    ).astype(F32).astype(BF16)
    acc_s[...] = jnp.zeros_like(acc_s)

    def lanes(j, width=LANES):
        return pl.ds(pl.multiple_of(j * width, width), width)

    def stack(value, mask):
        copies = mask.shape[0] // value.shape[0]
        return jnp.concatenate([value] * copies, axis=0) * mask

    def tokens_stack(value):
        mask = mask_tok[...]
        return jnp.concatenate(
            [stack(value[n * SUB : (n + 1) * SUB], mask) for n in range(subs)], axis=1
        )

    def carry_product(table, states):
        mask = mask_mode[...]
        split = [halves(s) for s in states]
        right = [
            jnp.concatenate([stack(s[k], mask) for s in split], axis=1) for k in range(2)
        ]
        out = product(halves(table), right)
        return jnp.concatenate(
            [out[:, n * LANES : (n + 1) * LANES] for n in range(subs)], axis=0
        )

    def put_state(ref, j, value):
        if per:
            ref[j // per, pl.ds(pl.multiple_of((j % per) * modes, modes), modes)] = value
        else:
            count = modes // piece_rows
            for q in range(count):
                ref[j * count + q] = value[q * piece_rows : (q + 1) * piece_rows]

    def take_state(ref, j):
        if per:
            return ref[j // per, pl.ds(pl.multiple_of((j % per) * modes, modes), modes)]
        count = modes // piece_rows
        return jnp.concatenate([ref[j * count + q] for q in range(count)], axis=0)

    def rate_wide(j):
        return wide_s[j, :modes, :wide]

    def res_wide(j):
        return wide_s[j, modes:, :wide]

    def chan_rate(j):
        return wide_s[j, :modes, wide:]

    def signal_of(j):
        at = lanes(j)
        return key_ref[:, at].astype(F32) * value_ref[:, at].astype(F32)

    def strided(row, first):
        parts = []
        for h in range(wide // LANES):
            part = jnp.broadcast_to(row[:, h * LANES : (h + 1) * LANES], (SUB, LANES))
            parts.append(pltpu.roll(part, first, 1, stride=1, stride_axis=0))
        return jnp.concatenate(parts, axis=1)

    def batch(compute, store, js):
        results = [compute(j) for j in js]
        for j, result in zip(js, results):
            store(j, *result)

    def batches(compute, store, first, last, size):
        def step(i, _):
            batch(compute, store, [first + i * size + b for b in range(size)])
            return 0

        lax.fori_loop(0, (last - first) // size, step, 0)

    def transfer(source, target, phase, d, by_target=True):
        there = lax.rem(here + d, ctx_count)
        return pltpu.make_async_remote_copy(
            src_ref=source.at[there] if by_target else source,
            dst_ref=target.at[here],
            send_sem=send_sem.at[phase, d],
            recv_sem=recv_sem.at[phase, d],
            device_id={"ctx": there},
            device_id_type=MESH,
        )

    def all_others(act):
        def step(d, _):
            act(d)
            return 0

        lax.fori_loop(1, ctx_count, step, 0)

    def blocks_then_send(compute, store, source, target, phase):
        if per:
            def step(d, _):
                piece = lax.rem(here + d, ctx_count)
                batch(compute, store, [piece * per + b for b in range(per)])
                transfer(source, target, phase, d).start()
                return 0

            lax.fori_loop(1, ctx_count, step, 0)
            batch(compute, store, [here * per + b for b in range(per)])
        else:
            batches(compute, store, 0, blocks, 2)
            all_others(lambda d: transfer(source, target, phase, d).start())
        target[here] = source[here]

    def receive_then_blocks(compute, store, source, target, phase):
        target[here] = source[here]
        if per:
            batch(compute, store, [here * per + b for b in range(per)])

            def step(d, _):
                transfer(source, target, phase, d).wait_recv()
                piece = lax.rem(here - d + ctx_count, ctx_count)
                batch(compute, store, [piece * per + b for b in range(per)])
                return 0

            lax.fori_loop(1, ctx_count, step, 0)
        else:
            all_others(lambda d: transfer(source, target, phase, d).wait_recv())
            batches(compute, store, 0, blocks, 2)

    def owned_decay():
        if per:
            rates = jnp.concatenate([chan_rate(here * per + b) for b in range(per)], axis=0)
            return jnp.exp(-length * rates)
        count = modes // piece_rows
        whole = chan_rate(here // count)
        rates = whole[:piece_rows]
        for q in range(1, count):
            rates = jnp.where(
                here % count == q, whole[q * piece_rows : (q + 1) * piece_rows], rates
            )
        return jnp.exp(-length * rates)

    def join(own, source, target, result, phase, reverse):
        decay = owned_decay()
        all_others(lambda d: transfer(own, source, phase, d).wait_recv())

        def step(k, state):
            at = ctx_count - 1 - k if reverse else k
            target[at] = state
            return decay * state + source[at]

        lax.fori_loop(0, ctx_count, step, jnp.zeros((piece_rows, LANES), F32), unroll=True)
        all_others(lambda d: transfer(target, result, phase + 1, d).start())

    eye = unit(groups)
    for load in loads[:2]:
        load.wait()
    tables = jnp.concatenate([jnp.exp(log_ref[...]), res_ref[...]], axis=0)
    rates, residues = transposed(tables[:modes], eye), transposed(tables[modes:], eye)
    spread_modes = (
        iota((modes, LANES), 0) == iota((modes, LANES), 1) % modes
    ).astype(F32).astype(BF16)
    own_row = iota((in_block, LANES), 0) == iota((in_block, LANES), 1) // modes
    rolled = [
        pltpu.roll(tables, (groups - j * in_block) % groups, 1) for j in range(blocks)
    ]
    wide_s[...] = exact_dot(jnp.concatenate(rolled, axis=0), widen[...]).reshape(wide_s.shape)
    flat = exact_dot(jnp.concatenate([rates, residues], axis=0), spread_modes)
    for q in range(2):
        for j in range(blocks):
            first = q * groups + j * in_block
            part = jnp.where(own_row, flat[first : first + in_block], 0.0)
            row_s[q, j : j + 1] = jnp.sum(part, axis=0, keepdims=True)

    row_id = iota((SUB, wide), 0)
    lane_id = iota((SUB, wide), 1) % SUB
    offset = (iota((modes, wide), 1) % SUB).astype(F32)
    time = iota((SUB, in_block * modes), 0).astype(F32)

    def states_of(j):
        ending = jnp.exp(-rate_wide(j) * (SUB - offset))
        table = jnp.concatenate([ending, ending * (SUB - offset)], axis=0)
        high, low = halves(signal_of(j))
        out = product(halves(table), (tokens_stack(high), tokens_stack(low)))
        step = jnp.exp(-chan_rate(j) * SUB)
        state = out[:modes, :LANES]
        for n in range(1, subs):
            state = step * state + out[:modes, n * LANES : (n + 1) * LANES]
        return out, state

    def states_put(j, out, state):
        sub_s[j] = out
        put_state(own_s, j, state)

    def local_of(j):
        taps = jnp.sum(
            res_wide(j) * jnp.exp(-rate_wide(j) * (SUB - 1.0 - offset)), axis=0, keepdims=True
        )
        toeplitz = jnp.where(lane_id <= row_id, strided(taps, LANES - SUB + 1), 0.0)
        signal = signal_of(j)
        high, low = halves(signal)
        out = product(halves(toeplitz), (tokens_stack(high), tokens_stack(low)))
        out = jnp.concatenate([out[:, n * LANES : (n + 1) * LANES] for n in range(subs)], axis=0)
        return (out + skip_ref[:, lanes(j)] * signal,)

    def local_put(j, out):
        mixed_s[:, lanes(j)] = out

    def carried_of(j):
        at = lanes(j)
        step = jnp.exp(-chan_rate(j) * SUB)
        state, moment = take_state(got_s, j), jnp.zeros((modes, LANES), F32)
        states, saved = [], []
        for n in range(subs):
            states.append(state)
            saved.append(jnp.concatenate([state, moment], axis=0))
            part = sub_s[j, :, n * LANES : (n + 1) * LANES]
            moment = step * (moment + SUB * state) + part[modes:]
            state = step * state + part[:modes]
        table = row_s[1, pl.ds(j, 1)] * jnp.exp(-row_s[0, pl.ds(j, 1)] * time)
        mixed = mixed_s[:, at] + carry_product(table, states)
        premix = gate_ref[:, at].astype(F32) * mixed
        pull = cot_ref[:, at].astype(F32) * gain_ref[:, at]
        return saved, moment, mixed, premix * premix, pull * premix

    def carried_put(j, saved, moment, mixed, square, inner):
        for n in range(subs):
            state_s[j, n] = saved[n]
        late_s[j] = moment
        mixed_s[:, lanes(j)] = mixed
        acc_s[0] += square
        acc_s[1] += inner

    for load in loads[2:4]:
        load.wait()
    pl.semaphore_wait(barrier, ctx_count - 1 + tp_count - 1)
    half = blocks // 2
    blocks_then_send(states_of, states_put, own_s, in_s, 0)
    loads[4].wait()
    batches(local_of, local_put, 0, half, 4)
    join(own_s, in_s, out_s, got_s, 0, False)
    batches(local_of, local_put, half, blocks, 4)
    for load in loads[5:]:
        load.wait()
    receive_then_blocks(carried_of, carried_put, out_s, got_s, 1)

    for k in range(2):
        row = jnp.sum(acc_s[k].T, axis=0, keepdims=True)
        norm_own[4 * k : 4 * k + 4] = jnp.broadcast_to(row, (4, length))
    copies = []
    for d in range(1, tp_count):
        copy = pltpu.make_async_remote_copy(
            src_ref=norm_own,
            dst_ref=norm_got.at[side],
            send_sem=tp_send.at[d],
            recv_sem=tp_recv.at[d],
            device_id={"tp": lax.rem(side + d, tp_count)},
            device_id_type=MESH,
        )
        copy.start()
        copies.append(copy)
    norm_got[side] = norm_own[...]

    def tables_of(j):
        start = jnp.exp(-rate_wide(j) * offset)
        taps = jnp.sum(res_wide(j) * start, axis=0, keepdims=True)
        toeplitz = jnp.where(lane_id >= row_id, strided(taps, 0), 0.0)
        return halves(jnp.concatenate([start, start * offset], axis=0)) + halves(toeplitz)

    def tables_put(j, high, low, toeplitz_high, toeplitz_low):
        table_s[j, 0], table_s[j, 1] = high, low
        toeplitz_s[j, 0], toeplitz_s[j, 1] = toeplitz_high, toeplitz_low

    batches(tables_of, tables_put, 0, blocks, 4)
    for copy in copies:
        copy.wait()
    sums = norm_got[0]
    for k in range(1, tp_count):
        sums = sums + norm_got[k]
    inverse_row = lax.rsqrt(sums[0:1] / full_width + EPSILON)
    inner_row = sums[4:5] * inverse_row / full_width
    acc_s[0] = jnp.broadcast_to(inverse_row, (LANES, length)).T
    acc_s[1] = jnp.broadcast_to(inner_row, (LANES, length)).T

    to_group = (
        iota((LANES, groups), 0) // members == iota((LANES, groups), 1)
    ).astype(F32).astype(BF16)
    wide_to_group = (
        iota((wide, groups), 0) // SUB == iota((wide, groups), 1)
    ).astype(F32).astype(BF16)
    half_row = iota((SUB, LANES), 0)

    def weight_of(j):
        at = lanes(j)
        inverse, inner = acc_s[0], acc_s[1]
        gate = gate_ref[:, at].astype(F32)
        normed = gate * mixed_s[:, at] * inverse
        dpre = (cot_ref[:, at].astype(F32) * gain_ref[:, at] - normed * inner) * inverse
        weight = dpre * gate
        high, low = halves(weight)
        out = product((table_s[j, 0], table_s[j, 1]), (tokens_stack(high), tokens_stack(low)))
        step = jnp.exp(-chan_rate(j) * SUB)
        state = out[:modes, (subs - 1) * LANES :]
        for n in range(subs - 2, -1, -1):
            state = step * state + out[:modes, n * LANES : (n + 1) * LANES]
        return weight, out, state

    def weight_put(j, weight, out, state):
        weight_s[:, lanes(j)] = weight
        sub_s[j] = out
        put_state(own_b, j, state)

    def inside_of(j):
        at = lanes(j)
        inverse, inner = acc_s[0], acc_s[1]
        mixed = mixed_s[:, at]
        gain = gain_ref[:, at]
        normed = gate_ref[:, at].astype(F32) * mixed * inverse
        dpre = (cot_ref[:, at].astype(F32) * gain - normed * inner) * inverse
        weight = weight_s[:, at]
        start = jnp.exp(-rate_wide(j) * offset)
        high, low = halves(weight)
        right = (tokens_stack(high), tokens_stack(low))
        back = product((toeplitz_s[j, 0], toeplitz_s[j, 1]), right)
        back = jnp.concatenate([back[:, n * LANES : (n + 1) * LANES] for n in range(subs)], axis=0)

        left = tuple(
            jnp.concatenate([part[n * SUB : (n + 1) * SUB] for n in range(subs)], axis=1)
            for part in halves(signal_of(j))
        )
        pairs = jnp.where(lane_id >= row_id, product(left, right, dot_t), 0.0)
        lagged = []
        for h in range(wide // LANES):
            part = pairs[:, h * LANES : (h + 1) * LANES]
            bit = 1
            while bit < SUB:
                moved = pltpu.roll(part, LANES - bit, 1)
                part = jnp.where((half_row // bit) % 2 == 1, moved, part)
                bit *= 2
            lagged.append(jnp.sum(part, axis=0, keepdims=True))
        zeroth = start * jnp.concatenate(lagged, axis=1)
        local = jnp.concatenate([zeroth, zeroth * offset], axis=0)

        cross = jnp.zeros((modes, LANES), F32)
        cross_moment = jnp.zeros((modes, LANES), F32)
        for n in range(subs):
            part = sub_s[j, :, n * LANES : (n + 1) * LANES]
            both = state_s[j, n]
            cross += part[:modes] * both[:modes]
            cross_moment += part[modes:] * both[:modes] + part[:modes] * both[modes:]
        return (
            (normed * gain).astype(BF16),
            (dpre * mixed).astype(BF16),
            back + skip_ref[:, at] * weight,
            local,
            jnp.concatenate([cross, cross_moment], axis=0),
        )

    def inside_put(j, mixer, grad_q, back, local, cross):
        at = lanes(j)
        mixer_ref[:, at] = mixer
        gq_ref[:, at] = grad_q
        back_s[:, at] = back
        local_s[j] = local
        cross_s[j] = cross

    def ending_of(j):
        return (cross_s[j, modes:] + take_state(got_b, j) * late_s[j],)

    def ending_put(j, moment):
        cross_s[j, modes:] = moment

    def group_sums(ref, ones):
        rows = exact_dot(ref[...].reshape(blocks * 2 * modes, ref.shape[2]), ones)
        total = rows[: 2 * modes]
        for j in range(1, blocks):
            total += pltpu.roll(rows[2 * modes * j : 2 * modes * (j + 1)], j * in_block, 1)
        return total

    def signal_grad_of(j):
        at = lanes(j)
        step = jnp.exp(-chan_rate(j) * SUB)
        state = take_state(got_b, j)
        states = []
        for n in range(subs - 1, -1, -1):
            states.append(state)
            state = step * state + sub_s[j, :modes, n * LANES : (n + 1) * LANES]
        states.reverse()
        table = row_s[1, pl.ds(j, 1)] * jnp.exp(-row_s[0, pl.ds(j, 1)] * (SUB - time))
        grad = back_s[:, at] + carry_product(table, states)
        return (
            (grad * value_ref[:, at].astype(F32)).astype(BF16),
            (grad * key_ref[:, at].astype(F32)).astype(BF16),
        )

    def signal_grad_put(j, grad_k, grad_v):
        gk_ref[:, lanes(j)] = grad_k
        gv_ref[:, lanes(j)] = grad_v

    blocks_then_send(weight_of, weight_put, own_b, in_b, 2)
    batches(inside_of, inside_put, 0, half, 2)
    join(own_b, in_b, out_b, got_b, 2, True)
    batches(inside_of, inside_put, half, blocks, 2)
    stores = [
        pltpu.make_async_copy(mixer_ref, mixer_out, store_sem.at[0]),
        pltpu.make_async_copy(gq_ref, gq_out, store_sem.at[1]),
    ]
    for store in stores:
        store.start()
    inside_total = group_sums(local_s, wide_to_group)
    receive_then_blocks(ending_of, ending_put, out_b, got_b, 3)
    part_s[...] = inside_total + group_sums(cross_s, to_group)
    all_others(lambda d: transfer(part_s, part_got, 4, d, False).start())
    part_got[here] = part_s[...]

    size = 4

    def grad_stores(i):
        at = lanes(i, size * LANES)
        return [
            pltpu.make_async_copy(source.at[:, at], target.at[:, at], part_sem.at[k, i])
            for k, (source, target) in enumerate(((gk_ref, gk_out), (gv_ref, gv_out)))
        ]

    def grads(i, _):
        batch(signal_grad_of, signal_grad_put, [i * size + b for b in range(size)])
        for store in grad_stores(i):
            store.start()
        return 0

    lax.fori_loop(0, blocks // size, grads, 0)
    all_others(lambda d: transfer(part_s, part_got, 4, d, False).wait())
    sums = part_got[0]
    for k in range(1, ctx_count):
        sums = sums + part_got[k]
    scale = 1.0 / (length * ctx_count)
    filt_ref[:modes] = sums[:modes] * scale
    filt_ref[modes:] = -res_ref[...] * jnp.exp(log_ref[...]) * sums[modes:] * scale
    last = [
        pltpu.make_async_copy(filt_ref.at[:modes], res_out, store_sem.at[2]),
        pltpu.make_async_copy(filt_ref.at[modes:], log_out, store_sem.at[3]),
    ]
    for store in last:
        store.start()

    def drain(d):
        for phase, (source, target) in enumerate(
            ((own_s, in_s), (out_s, got_s), (own_b, in_b), (out_b, got_b))
        ):
            transfer(source, target, phase, d).wait_send()

    all_others(drain)
    for i in range(blocks // size):
        stores += grad_stores(i)
    for store in stores + last:
        store.wait()


def finish(*refs):
    sources, targets, sems = refs[:6], refs[6:12], refs[12]
    copies = [
        pltpu.make_async_copy(source, target, sems.at[k])
        for k, (source, target) in enumerate(zip(sources, targets))
    ]
    for copy in copies:
        copy.start()
    for copy in copies:
        copy.wait()


def per_device(out_gate, key_proj, value_proj, residue, log_decay, skip, gain, cotangent):
    length, channels = out_gate.shape
    groups, modes = residue.shape
    members = channels // groups
    ctx_count, tp_count = lax.axis_size("ctx"), lax.axis_size("tp")
    blocks = channels // LANES
    in_block = LANES // members
    subs = length // SUB
    wide = in_block * SUB
    piece_rows = blocks * modes // ctx_count
    pieces = pltpu.VMEM((ctx_count, piece_rows, LANES), F32)
    wide_out = jax.ShapeDtypeStruct((length, channels), BF16)
    table_out = jax.ShapeDtypeStruct((modes, groups), F32)
    hbm = pl.BlockSpec(memory_space=pltpu.HBM)
    results = [wide_out] * 4 + [table_out] * 2
    computed = pl.pallas_call(
        functools.partial(kernel, ctx_count, tp_count, float(channels * tp_count)),
        out_shape=results,
        in_specs=[hbm] * 8,
        out_specs=[hbm] * 6,
        scratch_shapes=[
            pltpu.VMEM((length, channels), BF16),
            pltpu.VMEM((length, channels), BF16),
            pltpu.VMEM((length, channels), BF16),
            pltpu.VMEM((length, channels), BF16),
            pltpu.VMEM((1, channels), F32),
            pltpu.VMEM((1, channels), F32),
            pltpu.VMEM((modes, groups), F32),
            pltpu.VMEM((modes, groups), F32),
            pltpu.VMEM((length, channels), BF16),
            pltpu.VMEM((length, channels), BF16),
            pltpu.VMEM((length, channels), BF16),
            pltpu.VMEM((length, channels), BF16),
            pltpu.VMEM((2 * modes, groups), F32),
            pltpu.VMEM((length, channels), F32),
            pltpu.VMEM((length, channels), F32),
            pltpu.VMEM((length, channels), F32),
            pltpu.VMEM((blocks, 2 * modes, subs * LANES), F32),
            pltpu.VMEM((blocks, subs, 2 * modes, LANES), F32),
            pltpu.VMEM((blocks, modes, LANES), F32),
            pltpu.VMEM((wide, LANES), BF16),
            pltpu.VMEM((in_block * modes, LANES), BF16),
            pltpu.VMEM((groups, wide + LANES), BF16),
            pltpu.VMEM((blocks, 2 * modes, wide + LANES), F32),
            pltpu.VMEM((blocks, 2, 2 * modes, wide), BF16),
            pltpu.VMEM((blocks, 2, SUB, wide), BF16),
            pltpu.VMEM((blocks, 2 * modes, wide), F32),
            pltpu.VMEM((blocks, 2 * modes, LANES), F32),
            pltpu.VMEM((2, blocks, LANES), F32),
            pltpu.VMEM((2, length, LANES), F32),
            pieces, pieces, pieces, pieces,
            pieces, pieces, pieces, pieces,
            pltpu.VMEM((8, length), F32),
            pltpu.VMEM((tp_count, 8, length), F32),
            pltpu.VMEM((2 * modes, groups), F32),
            pltpu.VMEM((ctx_count, 2 * modes, groups), F32),
            pltpu.SemaphoreType.DMA((5, ctx_count)),
            pltpu.SemaphoreType.DMA((5, ctx_count)),
            pltpu.SemaphoreType.DMA((tp_count,)),
            pltpu.SemaphoreType.DMA((tp_count,)),
            pltpu.SemaphoreType.DMA((8,)),
            pltpu.SemaphoreType.DMA((4,)),
            pltpu.SemaphoreType.DMA((2, blocks)),
        ],
        compiler_params=pltpu.CompilerParams(
            collective_id=0, has_side_effects=True, vmem_limit_bytes=60 * 1024 * 1024
        ),
        name="mixer",
    )(out_gate, key_proj, value_proj, cotangent, skip[None], gain[None], residue.T, log_decay.T)
    *wide_results, grad_residue, grad_log_decay = pl.pallas_call(
        finish,
        out_shape=results,
        in_specs=[hbm] * 6,
        out_specs=[hbm] * 6,
        scratch_shapes=[pltpu.SemaphoreType.DMA((6,))],
        compiler_params=pltpu.CompilerParams(vmem_limit_bytes=60 * 1024 * 1024),
        name="finish",
    )(*computed)
    return *wide_results, grad_residue.T, grad_log_decay.T


def solution(mesh):
    wide, table, row = P("ctx", "tp"), P("tp", None), P("tp")
    return jax.shard_map(
        per_device,
        mesh=mesh,
        in_specs=(wide, wide, wide, table, table, row, row, wide),
        out_specs=(wide, wide, wide, wide, table, table),
        check_vma=False,
    )
```

```python
import functools

import jax
import jax.numpy as jnp
from jax import lax
from jax.experimental import pallas as pl
from jax.experimental.pallas import tpu as pltpu
from jax.sharding import PartitionSpec as P

EPSILON = 1e-06
LANES = 128
SUB = 32
PART_ROWS = 64
F32 = jnp.float32
BF16 = jnp.bfloat16
MESH = pl.DeviceIdType.MESH


def halves(value):
    high = value.astype(BF16)
    return high, (value - high.astype(F32)).astype(BF16)


def dot(a, b):
    return jnp.dot(a, b, preferred_element_type=F32)


def dot_t(a, b):
    return lax.dot_general(a, b, (((1,), (1,)), ((), ())), preferred_element_type=F32)


def product(left, right, multiply=dot):
    rows = left[0].shape[0]
    both = multiply(jnp.concatenate(left, axis=0), right[0])
    return both[:rows] + both[rows:] + multiply(left[0], right[1])


def exact_dot(value, ones):
    rows = value.shape[0]
    high, rest = value.astype(BF16), None
    rest = value - high.astype(F32)
    mid = rest.astype(BF16)
    low = (rest - mid.astype(F32)).astype(BF16)
    out = dot(jnp.concatenate([high, mid, low], axis=0), ones)
    return out[:rows] + out[rows : 2 * rows] + out[2 * rows :]


def iota(shape, dim):
    return lax.broadcasted_iota(jnp.int32, shape, dim)


def transposed(value, eye):
    high = value.astype(BF16)
    rest = value - high.astype(F32)
    mid = rest.astype(BF16)
    low = (rest - mid.astype(F32)).astype(BF16)
    return dot_t(eye, high) + dot_t(eye, mid) + dot_t(eye, low)


def unit(size):
    return (iota((size, size), 0) == iota((size, size), 1)).astype(F32).astype(BF16)


def kernel(
    ctx_count,
    tp_count,
    full_width,
    gate_in,
    key_in,
    value_in,
    cot_in,
    skip_in,
    gain_in,
    res_in,
    log_in,
    mixer_out,
    gq_out,
    gk_out,
    gv_out,
    res_out,
    log_out,
    gate_ref,
    key_ref,
    value_ref,
    cot_ref,
    skip_ref,
    gain_ref,
    res_ref,
    log_ref,
    mixer_ref,
    gq_ref,
    gk_ref,
    gv_ref,
    filt_ref,
    mixed_s,
    weight_s,
    back_s,
    sub_s,
    state_s,
    late_s,
    mask_tok,
    mask_mode,
    widen,
    wide_s,
    table_s,
    toeplitz_s,
    turned_s,
    local_s,
    cross_s,
    row_s,
    acc_s,
    own_s,
    in_s,
    out_s,
    got_s,
    own_b,
    in_b,
    out_b,
    got_b,
    norm_own,
    norm_got,
    part_s,
    part_got,
    send_sem,
    recv_sem,
    tp_send,
    tp_recv,
    load_sem,
    store_sem,
    part_sem,
):
    here = lax.axis_index("ctx")
    side = lax.axis_index("tp")
    length, channels = gate_ref.shape
    modes, groups = res_ref.shape
    members = channels // groups
    subs = length // SUB
    blocks = channels // LANES
    in_block = LANES // members
    wide = in_block * SUB
    piece_rows = blocks * modes // ctx_count
    per = piece_rows // modes

    loads = [
        pltpu.make_async_copy(source, target, load_sem.at[k])
        for k, (source, target) in enumerate(
            (
                (res_in, res_ref),
                (log_in, log_ref),
                (key_in, key_ref),
                (value_in, value_ref),
                (skip_in, skip_ref),
                (gate_in, gate_ref),
                (cot_in, cot_ref),
                (gain_in, gain_ref),
            )
        )
    ]
    for load in loads:
        load.start()

    barrier = pltpu.get_barrier_semaphore()
    for d in range(1, ctx_count):
        pl.semaphore_signal(
            barrier, inc=1, device_id={"ctx": lax.rem(here + d, ctx_count)}, device_id_type=MESH
        )
    for d in range(1, tp_count):
        pl.semaphore_signal(
            barrier, inc=1, device_id={"tp": lax.rem(side + d, tp_count)}, device_id_type=MESH
        )

    mask_tok[...] = (
        iota((wide, LANES), 0) // SUB == iota((wide, LANES), 1) // members
    ).astype(F32).astype(BF16)
    mask_mode[...] = (
        iota((in_block * modes, LANES), 0) // modes == iota((in_block * modes, LANES), 1) // members
    ).astype(F32).astype(BF16)
    widen[:, :wide] = (iota((groups, wide), 0) == iota((groups, wide), 1) // SUB).astype(F32).astype(BF16)
    widen[:, wide:] = (
        iota((groups, LANES), 0) == iota((groups, LANES), 1) // members
    ).astype(F32).astype(BF16)
    acc_s[...] = jnp.zeros_like(acc_s)

    def lanes(j, width=LANES):
        return pl.ds(pl.multiple_of(j * width, width), width)

    def stack(value, mask):
        copies = mask.shape[0] // value.shape[0]
        return jnp.concatenate([value] * copies, axis=0) * mask

    def tokens_stack(value):
        mask = mask_tok[...]
        return jnp.concatenate(
            [stack(value[n * SUB : (n + 1) * SUB], mask) for n in range(subs)], axis=1
        )

    def carry_product(table, states):
        mask = mask_mode[...]
        split = [halves(s) for s in states]
        right = [
            jnp.concatenate([stack(s[k], mask) for s in split], axis=1) for k in range(2)
        ]
        out = product(halves(table), right)
        return jnp.concatenate(
            [out[:, n * LANES : (n + 1) * LANES] for n in range(subs)], axis=0
        )

    def put_state(ref, j, value):
        if per:
            ref[j // per, pl.ds(pl.multiple_of((j % per) * modes, modes), modes)] = value
        else:
            count = modes // piece_rows
            for q in range(count):
                ref[j * count + q] = value[q * piece_rows : (q + 1) * piece_rows]

    def take_state(ref, j):
        if per:
            return ref[j // per, pl.ds(pl.multiple_of((j % per) * modes, modes), modes)]
        count = modes // piece_rows
        return jnp.concatenate([ref[j * count + q] for q in range(count)], axis=0)

    def rate_wide(j):
        return wide_s[j, :modes, :wide]

    def res_wide(j):
        return wide_s[j, modes:, :wide]

    def chan_rate(j):
        return wide_s[j, :modes, wide:]

    def signal_of(j):
        at = lanes(j)
        return key_ref[:, at].astype(F32) * value_ref[:, at].astype(F32)

    def strided(row, first):
        parts = []
        for h in range(wide // LANES):
            part = jnp.broadcast_to(row[:, h * LANES : (h + 1) * LANES], (SUB, LANES))
            parts.append(pltpu.roll(part, first, 1, stride=1, stride_axis=0))
        return jnp.concatenate(parts, axis=1)

    def batch(compute, store, js):
        results = [compute(j) for j in js]
        for j, result in zip(js, results):
            store(j, *result)

    def batches(compute, store, first, last, size):
        def step(i, _):
            batch(compute, store, [first + i * size + b for b in range(size)])
            return 0

        lax.fori_loop(0, (last - first) // size, step, 0)

    def transfer(source, target, phase, d, by_target=True):
        there = lax.rem(here + d, ctx_count)
        return pltpu.make_async_remote_copy(
            src_ref=source.at[there] if by_target else source,
            dst_ref=target.at[here],
            send_sem=send_sem.at[phase, d],
            recv_sem=recv_sem.at[phase, d],
            device_id={"ctx": there},
            device_id_type=MESH,
        )

    def all_others(act):
        def step(d, _):
            act(d)
            return 0

        lax.fori_loop(1, ctx_count, step, 0)

    pair = 2 if ctx_count % 2 == 0 else 1

    def piece_blocks(piece):
        return [piece * per + b for b in range(per)]

    def blocks_then_send(compute, store, source, target, phase):
        if per:
            def step(i, _):
                first = i * pair + 1
                batch(
                    compute,
                    store,
                    [
                        j
                        for b in range(pair)
                        for j in piece_blocks(lax.rem(here + first + b, ctx_count))
                    ],
                )
                for b in range(pair):
                    @pl.when(first + b < ctx_count)
                    def _():
                        transfer(source, target, phase, first + b).start()

                return 0

            lax.fori_loop(0, ctx_count // pair, step, 0)
        else:
            batches(compute, store, 0, blocks, 2)
            all_others(lambda d: transfer(source, target, phase, d).start())
        target[here] = source[here]

    def receive_then_blocks(compute, store, source, target, phase):
        target[here] = source[here]
        if per:
            def step(i, _):
                first = i * pair
                for b in range(pair):
                    @pl.when(first + b > 0)
                    def _():
                        transfer(source, target, phase, first + b).wait_recv()

                batch(
                    compute,
                    store,
                    [
                        j
                        for b in range(pair)
                        for j in piece_blocks(lax.rem(here - first - b + ctx_count, ctx_count))
                    ],
                )
                return 0

            lax.fori_loop(0, ctx_count // pair, step, 0)
        else:
            all_others(lambda d: transfer(source, target, phase, d).wait_recv())
            batches(compute, store, 0, blocks, 2)

    def owned_decay():
        if per:
            rates = jnp.concatenate([chan_rate(here * per + b) for b in range(per)], axis=0)
            return jnp.exp(-length * rates)
        count = modes // piece_rows
        whole = chan_rate(here // count)
        rates = whole[:piece_rows]
        for q in range(1, count):
            rates = jnp.where(
                here % count == q, whole[q * piece_rows : (q + 1) * piece_rows], rates
            )
        return jnp.exp(-length * rates)

    def join(own, source, target, result, phase, reverse):
        decay = owned_decay()
        all_others(lambda d: transfer(own, source, phase, d).wait_recv())

        def step(k, state):
            at = ctx_count - 1 - k if reverse else k
            target[at] = state
            return decay * state + source[at]

        lax.fori_loop(0, ctx_count, step, jnp.zeros((piece_rows, LANES), F32), unroll=True)
        all_others(lambda d: transfer(target, result, phase + 1, d).start())

    eye = unit(groups)
    for load in loads[:2]:
        load.wait()
    tables = jnp.concatenate([jnp.exp(log_ref[...]), res_ref[...]], axis=0)
    rates, residues = transposed(tables[:modes], eye), transposed(tables[modes:], eye)
    spread_modes = (
        iota((modes, LANES), 0) == iota((modes, LANES), 1) % modes
    ).astype(F32).astype(BF16)
    own_row = iota((in_block, LANES), 0) == iota((in_block, LANES), 1) // modes
    rolled = [
        pltpu.roll(tables, (groups - j * in_block) % groups, 1) for j in range(blocks)
    ]
    wide_s[...] = exact_dot(jnp.concatenate(rolled, axis=0), widen[...]).reshape(wide_s.shape)
    flat = exact_dot(jnp.concatenate([rates, residues], axis=0), spread_modes)
    for q in range(2):
        for j in range(blocks):
            first = q * groups + j * in_block
            part = jnp.where(own_row, flat[first : first + in_block], 0.0)
            row_s[q, j : j + 1] = jnp.sum(part, axis=0, keepdims=True)

    row_id = iota((SUB, wide), 0)
    lane_id = iota((SUB, wide), 1) % SUB
    offset = (iota((modes, wide), 1) % SUB).astype(F32)
    time = iota((SUB, in_block * modes), 0).astype(F32)

    def states_of(j):
        ending = jnp.exp(-rate_wide(j) * (SUB - offset))
        table = jnp.concatenate([ending, ending * (SUB - offset)], axis=0)
        high, low = halves(signal_of(j))
        out = product(halves(table), (tokens_stack(high), tokens_stack(low)))
        step = jnp.exp(-chan_rate(j) * SUB)
        state = out[:modes, :LANES]
        for n in range(1, subs):
            state = step * state + out[:modes, n * LANES : (n + 1) * LANES]
        return out, state

    def states_put(j, out, state):
        sub_s[j] = out
        put_state(own_s, j, state)

    def local_of(j):
        taps = jnp.sum(
            res_wide(j) * jnp.exp(-rate_wide(j) * (SUB - 1.0 - offset)), axis=0, keepdims=True
        )
        toeplitz = jnp.where(lane_id <= row_id, strided(taps, LANES - SUB + 1), 0.0)
        signal = signal_of(j)
        high, low = halves(signal)
        out = product(halves(toeplitz), (tokens_stack(high), tokens_stack(low)))
        out = jnp.concatenate([out[:, n * LANES : (n + 1) * LANES] for n in range(subs)], axis=0)
        return (out + skip_ref[:, lanes(j)] * signal,)

    def local_put(j, out):
        mixed_s[:, lanes(j)] = out

    def carried_of(j):
        at = lanes(j)
        step = jnp.exp(-chan_rate(j) * SUB)
        state, moment = take_state(got_s, j), jnp.zeros((modes, LANES), F32)
        states, saved = [], []
        for n in range(subs):
            states.append(state)
            saved.append(jnp.concatenate([state, moment], axis=0))
            part = sub_s[j, :, n * LANES : (n + 1) * LANES]
            moment = step * (moment + SUB * state) + part[modes:]
            state = step * state + part[:modes]
        table = row_s[1, pl.ds(j, 1)] * jnp.exp(-row_s[0, pl.ds(j, 1)] * time)
        mixed = mixed_s[:, at] + carry_product(table, states)
        premix = gate_ref[:, at].astype(F32) * mixed
        pull = cot_ref[:, at].astype(F32) * gain_ref[:, at]
        return saved, moment, mixed, premix * premix, pull * premix

    def carried_put(j, saved, moment, mixed, square, inner):
        for n in range(subs):
            state_s[j, n] = saved[n]
        late_s[j] = moment
        mixed_s[:, lanes(j)] = mixed
        acc_s[0] += square
        acc_s[1] += inner

    for load in loads[2:4]:
        load.wait()
    pl.semaphore_wait(barrier, ctx_count - 1 + tp_count - 1)
    half = blocks // 2
    blocks_then_send(states_of, states_put, own_s, in_s, 0)
    loads[4].wait()
    batches(local_of, local_put, 0, half, 4)
    join(own_s, in_s, out_s, got_s, 0, False)
    batches(local_of, local_put, half, blocks, 4)
    for load in loads[5:]:
        load.wait()
    receive_then_blocks(carried_of, carried_put, out_s, got_s, 1)

    for k in range(2):
        row = jnp.sum(acc_s[k].T, axis=0, keepdims=True)
        norm_own[4 * k : 4 * k + 4] = jnp.broadcast_to(row, (4, length))
    copies = []
    for d in range(1, tp_count):
        copy = pltpu.make_async_remote_copy(
            src_ref=norm_own,
            dst_ref=norm_got.at[side],
            send_sem=tp_send.at[d],
            recv_sem=tp_recv.at[d],
            device_id={"tp": lax.rem(side + d, tp_count)},
            device_id_type=MESH,
        )
        copy.start()
        copies.append(copy)
    norm_got[side] = norm_own[...]

    turn = (iota((SUB, SUB), 0) + iota((SUB, SUB), 1) == SUB - 1).astype(F32).astype(BF16)

    def tables_of(j):
        start = jnp.exp(-rate_wide(j) * offset)
        taps = jnp.sum(res_wide(j) * start, axis=0, keepdims=True)
        toeplitz = jnp.where(lane_id >= row_id, strided(taps, 0), 0.0)
        turned = tuple(
            dot(
                turn,
                jnp.concatenate([part[n * SUB : (n + 1) * SUB] for n in range(subs)], axis=1),
            ).astype(BF16)
            for part in halves(signal_of(j))
        )
        return (
            halves(jnp.concatenate([start, start * offset], axis=0)) + halves(toeplitz) + turned
        )

    def tables_put(j, high, low, toeplitz_high, toeplitz_low, turned_high, turned_low):
        turned_s[j, 0], turned_s[j, 1] = turned_high, turned_low
        table_s[j, 0], table_s[j, 1] = high, low
        toeplitz_s[j, 0], toeplitz_s[j, 1] = toeplitz_high, toeplitz_low

    batches(tables_of, tables_put, 0, blocks, 4)
    for copy in copies:
        copy.wait()
    sums = norm_got[0]
    for k in range(1, tp_count):
        sums = sums + norm_got[k]
    inverse_row = lax.rsqrt(sums[0:1] / full_width + EPSILON)
    inner_row = sums[4:5] * inverse_row / full_width
    acc_s[0] = jnp.broadcast_to(inverse_row, (LANES, length)).T
    acc_s[1] = jnp.broadcast_to(inner_row, (LANES, length)).T

    to_group = (
        iota((LANES, groups), 0) // members == iota((LANES, groups), 1)
    ).astype(F32).astype(BF16)
    wide_to_group = (
        iota((wide, groups), 0) // SUB == iota((wide, groups), 1)
    ).astype(F32).astype(BF16)

    def weight_of(j):
        at = lanes(j)
        inverse, inner = acc_s[0], acc_s[1]
        gate = gate_ref[:, at].astype(F32)
        normed = gate * mixed_s[:, at] * inverse
        dpre = (cot_ref[:, at].astype(F32) * gain_ref[:, at] - normed * inner) * inverse
        weight = dpre * gate
        high, low = halves(weight)
        out = product((table_s[j, 0], table_s[j, 1]), (tokens_stack(high), tokens_stack(low)))
        step = jnp.exp(-chan_rate(j) * SUB)
        state = out[:modes, (subs - 1) * LANES :]
        for n in range(subs - 2, -1, -1):
            state = step * state + out[:modes, n * LANES : (n + 1) * LANES]
        return weight, out, state

    def weight_put(j, weight, out, state):
        weight_s[:, lanes(j)] = weight
        sub_s[j] = out
        put_state(own_b, j, state)

    def inside_of(j):
        at = lanes(j)
        inverse, inner = acc_s[0], acc_s[1]
        mixed = mixed_s[:, at]
        gain = gain_ref[:, at]
        normed = gate_ref[:, at].astype(F32) * mixed * inverse
        dpre = (cot_ref[:, at].astype(F32) * gain - normed * inner) * inverse
        weight = weight_s[:, at]
        start = jnp.exp(-rate_wide(j) * offset)
        high, low = halves(weight)
        right = (tokens_stack(high), tokens_stack(low))
        back = product((toeplitz_s[j, 0], toeplitz_s[j, 1]), right)
        back = jnp.concatenate([back[:, n * LANES : (n + 1) * LANES] for n in range(subs)], axis=0)

        pairs = product((turned_s[j, 0], turned_s[j, 1]), right, dot_t)
        pairs = jnp.where(lane_id + row_id >= SUB - 1, pairs, 0.0)
        lagged = [
            jnp.sum(
                pltpu.roll(
                    pairs[:, h * LANES : (h + 1) * LANES], LANES - SUB + 1, 1, stride=1, stride_axis=0
                ),
                axis=0,
                keepdims=True,
            )
            for h in range(wide // LANES)
        ]
        zeroth = start * jnp.concatenate(lagged, axis=1)
        local = jnp.concatenate([zeroth, zeroth * offset], axis=0)

        cross = jnp.zeros((modes, LANES), F32)
        cross_moment = jnp.zeros((modes, LANES), F32)
        for n in range(subs):
            part = sub_s[j, :, n * LANES : (n + 1) * LANES]
            both = state_s[j, n]
            cross += part[:modes] * both[:modes]
            cross_moment += part[modes:] * both[:modes] + part[:modes] * both[modes:]
        return (
            (normed * gain).astype(BF16),
            (dpre * mixed).astype(BF16),
            back + skip_ref[:, at] * weight,
            local,
            jnp.concatenate([cross, cross_moment], axis=0),
        )

    def inside_put(j, mixer, grad_q, back, local, cross):
        at = lanes(j)
        mixer_ref[:, at] = mixer
        gq_ref[:, at] = grad_q
        back_s[:, at] = back
        local_s[j] = local
        cross_s[j] = cross

    def ending_of(j):
        return (cross_s[j, modes:] + take_state(got_b, j) * late_s[j],)

    def ending_put(j, moment):
        cross_s[j, modes:] = moment

    def group_sums(ref, ones):
        rows = exact_dot(ref[...].reshape(blocks * 2 * modes, ref.shape[2]), ones)
        total = rows[: 2 * modes]
        for j in range(1, blocks):
            total += pltpu.roll(rows[2 * modes * j : 2 * modes * (j + 1)], j * in_block, 1)
        return total

    def signal_grad_of(j):
        at = lanes(j)
        step = jnp.exp(-chan_rate(j) * SUB)
        state = take_state(got_b, j)
        states = []
        for n in range(subs - 1, -1, -1):
            states.append(state)
            state = step * state + sub_s[j, :modes, n * LANES : (n + 1) * LANES]
        states.reverse()
        table = row_s[1, pl.ds(j, 1)] * jnp.exp(-row_s[0, pl.ds(j, 1)] * (SUB - time))
        grad = back_s[:, at] + carry_product(table, states)
        return (
            (grad * value_ref[:, at].astype(F32)).astype(BF16),
            (grad * key_ref[:, at].astype(F32)).astype(BF16),
        )

    def signal_grad_put(j, grad_k, grad_v):
        gk_ref[:, lanes(j)] = grad_k
        gv_ref[:, lanes(j)] = grad_v

    blocks_then_send(weight_of, weight_put, own_b, in_b, 2)
    batches(inside_of, inside_put, 0, half, 4)
    join(own_b, in_b, out_b, got_b, 2, True)
    batches(inside_of, inside_put, half, blocks, 4)
    stores = [
        pltpu.make_async_copy(mixer_ref, mixer_out, store_sem.at[0]),
        pltpu.make_async_copy(gq_ref, gq_out, store_sem.at[1]),
    ]
    for store in stores:
        store.start()
    inside_total = group_sums(local_s, wide_to_group)
    receive_then_blocks(ending_of, ending_put, out_b, got_b, 3)
    part_s[...] = inside_total + group_sums(cross_s, to_group)
    all_others(lambda d: transfer(part_s, part_got, 4, d, False).start())
    part_got[here] = part_s[...]

    size = 4

    def grad_stores(i):
        at = lanes(i, size * LANES)
        return [
            pltpu.make_async_copy(source.at[:, at], target.at[:, at], part_sem.at[k, i])
            for k, (source, target) in enumerate(((gk_ref, gk_out), (gv_ref, gv_out)))
        ]

    def grads(i, _):
        batch(signal_grad_of, signal_grad_put, [i * size + b for b in range(size)])
        for store in grad_stores(i):
            store.start()
        return 0

    lax.fori_loop(0, blocks // size, grads, 0)
    all_others(lambda d: transfer(part_s, part_got, 4, d, False).wait())
    sums = part_got[0]
    for k in range(1, ctx_count):
        sums = sums + part_got[k]
    scale = 1.0 / (length * ctx_count)
    filt_ref[:modes] = sums[:modes] * scale
    filt_ref[modes:] = -res_ref[...] * jnp.exp(log_ref[...]) * sums[modes:] * scale
    last = [
        pltpu.make_async_copy(filt_ref.at[:modes], res_out, store_sem.at[2]),
        pltpu.make_async_copy(filt_ref.at[modes:], log_out, store_sem.at[3]),
    ]
    for store in last:
        store.start()

    def drain(d):
        for phase, (source, target) in enumerate(
            ((own_s, in_s), (out_s, got_s), (own_b, in_b), (out_b, got_b))
        ):
            transfer(source, target, phase, d).wait_send()

    all_others(drain)
    for i in range(blocks // size):
        stores += grad_stores(i)
    for store in stores + last:
        store.wait()


def finish(*refs):
    sources, targets, held, (load_sem, store_sem) = refs[:6], refs[6:12], refs[12:18], refs[18:]
    loads, stores = [], []
    for k, (source, target, middle) in enumerate(zip(sources, targets, held)):
        rows = min(source.shape[0], PART_ROWS)
        for q in range(source.shape[0] // rows):
            at = pl.ds(q * rows, rows)
            loads.append(pltpu.make_async_copy(source.at[at], middle.at[at], load_sem.at[k, q]))
            stores.append(pltpu.make_async_copy(middle.at[at], target.at[at], store_sem.at[k, q]))
    for load in loads:
        load.start()
    for load, store in zip(loads, stores):
        load.wait()
        store.start()
    for store in stores:
        store.wait()


def per_device(out_gate, key_proj, value_proj, residue, log_decay, skip, gain, cotangent):
    length, channels = out_gate.shape
    groups, modes = residue.shape
    members = channels // groups
    ctx_count, tp_count = lax.axis_size("ctx"), lax.axis_size("tp")
    blocks = channels // LANES
    in_block = LANES // members
    subs = length // SUB
    wide = in_block * SUB
    piece_rows = blocks * modes // ctx_count
    pieces = pltpu.VMEM((ctx_count, piece_rows, LANES), F32)
    wide_out = jax.ShapeDtypeStruct((length, channels), BF16)
    table_out = jax.ShapeDtypeStruct((modes, groups), F32)
    hbm = pl.BlockSpec(memory_space=pltpu.HBM)
    results = [wide_out] * 4 + [table_out] * 2
    computed = pl.pallas_call(
        functools.partial(kernel, ctx_count, tp_count, float(channels * tp_count)),
        out_shape=results,
        in_specs=[hbm] * 8,
        out_specs=[hbm] * 6,
        scratch_shapes=[
            pltpu.VMEM((length, channels), BF16),
            pltpu.VMEM((length, channels), BF16),
            pltpu.VMEM((length, channels), BF16),
            pltpu.VMEM((length, channels), BF16),
            pltpu.VMEM((1, channels), F32),
            pltpu.VMEM((1, channels), F32),
            pltpu.VMEM((modes, groups), F32),
            pltpu.VMEM((modes, groups), F32),
            pltpu.VMEM((length, channels), BF16),
            pltpu.VMEM((length, channels), BF16),
            pltpu.VMEM((length, channels), BF16),
            pltpu.VMEM((length, channels), BF16),
            pltpu.VMEM((2 * modes, groups), F32),
            pltpu.VMEM((length, channels), F32),
            pltpu.VMEM((length, channels), F32),
            pltpu.VMEM((length, channels), F32),
            pltpu.VMEM((blocks, 2 * modes, subs * LANES), F32),
            pltpu.VMEM((blocks, subs, 2 * modes, LANES), F32),
            pltpu.VMEM((blocks, modes, LANES), F32),
            pltpu.VMEM((wide, LANES), BF16),
            pltpu.VMEM((in_block * modes, LANES), BF16),
            pltpu.VMEM((groups, wide + LANES), BF16),
            pltpu.VMEM((blocks, 2 * modes, wide + LANES), F32),
            pltpu.VMEM((blocks, 2, 2 * modes, wide), BF16),
            pltpu.VMEM((blocks, 2, SUB, wide), BF16),
            pltpu.VMEM((blocks, 2, SUB, subs * LANES), BF16),
            pltpu.VMEM((blocks, 2 * modes, wide), F32),
            pltpu.VMEM((blocks, 2 * modes, LANES), F32),
            pltpu.VMEM((2, blocks, LANES), F32),
            pltpu.VMEM((2, length, LANES), F32),
            pieces, pieces, pieces, pieces,
            pieces, pieces, pieces, pieces,
            pltpu.VMEM((8, length), F32),
            pltpu.VMEM((tp_count, 8, length), F32),
            pltpu.VMEM((2 * modes, groups), F32),
            pltpu.VMEM((ctx_count, 2 * modes, groups), F32),
            pltpu.SemaphoreType.DMA((5, ctx_count)),
            pltpu.SemaphoreType.DMA((5, ctx_count)),
            pltpu.SemaphoreType.DMA((tp_count,)),
            pltpu.SemaphoreType.DMA((tp_count,)),
            pltpu.SemaphoreType.DMA((8,)),
            pltpu.SemaphoreType.DMA((4,)),
            pltpu.SemaphoreType.DMA((2, blocks)),
        ],
        compiler_params=pltpu.CompilerParams(
            collective_id=0, has_side_effects=True, vmem_limit_bytes=60 * 1024 * 1024
        ),
        name="mixer",
    )(out_gate, key_proj, value_proj, cotangent, skip[None], gain[None], residue.T, log_decay.T)
    *wide_results, grad_residue, grad_log_decay = pl.pallas_call(
        finish,
        out_shape=results,
        in_specs=[hbm] * 6,
        out_specs=[hbm] * 6,
        scratch_shapes=[pltpu.VMEM(result.shape, result.dtype) for result in results]
        + [pltpu.SemaphoreType.DMA((6, length // PART_ROWS))] * 2,
        compiler_params=pltpu.CompilerParams(vmem_limit_bytes=60 * 1024 * 1024),
        name="finish",
    )(*computed)
    return *wide_results, grad_residue.T, grad_log_decay.T


def solution(mesh):
    wide, table, row = P("ctx", "tp"), P("tp", None), P("tp")
    return jax.shard_map(
        per_device,
        mesh=mesh,
        in_specs=(wide, wide, wide, table, table, row, row, wide),
        out_specs=(wide, wide, wide, wide, table, table),
        check_vma=False,
    )
```

```python
import functools

import jax
import jax.numpy as jnp
from jax import lax
from jax.experimental import pallas as pl
from jax.experimental.pallas import tpu as pltpu
from jax.sharding import PartitionSpec as P

EPSILON = 1e-06
LANES = 128
SUB = 32
PART_ROWS = 64
F32 = jnp.float32
BF16 = jnp.bfloat16
MESH = pl.DeviceIdType.MESH


def halves(value):
    high = value.astype(BF16)
    return high, (value - high.astype(F32)).astype(BF16)


def dot(a, b):
    return jnp.dot(a, b, preferred_element_type=F32)


def dot_t(a, b):
    return lax.dot_general(a, b, (((1,), (1,)), ((), ())), preferred_element_type=F32)


def product(left, right, multiply=dot):
    rows = left[0].shape[0]
    both = multiply(jnp.concatenate(left, axis=0), right[0])
    return both[:rows] + both[rows:] + multiply(left[0], right[1])


def ones_dot(value, ones):
    rows = value.shape[0]
    out = dot(jnp.concatenate(halves(value), axis=0), ones)
    return out[:rows] + out[rows:]


def iota(shape, dim):
    return lax.broadcasted_iota(jnp.int32, shape, dim)


def transposed(value, eye):
    high = value.astype(BF16)
    rest = value - high.astype(F32)
    mid = rest.astype(BF16)
    low = (rest - mid.astype(F32)).astype(BF16)
    return dot_t(eye, high) + dot_t(eye, mid) + dot_t(eye, low)


def unit(size):
    return (iota((size, size), 0) == iota((size, size), 1)).astype(F32).astype(BF16)


def kernel(
    ctx_count,
    tp_count,
    full_width,
    gate_in,
    key_in,
    value_in,
    cot_in,
    skip_in,
    gain_in,
    res_in,
    log_in,
    mixer_out,
    gq_out,
    gk_out,
    gv_out,
    res_out,
    log_out,
    gate_ref,
    key_ref,
    value_ref,
    cot_ref,
    skip_ref,
    gain_ref,
    res_ref,
    log_ref,
    mixer_ref,
    gq_ref,
    gk_ref,
    gv_ref,
    filt_ref,
    mixed_s,
    weight_s,
    back_s,
    sub_s,
    state_s,
    late_s,
    mask_tok,
    mask_mode,
    widen,
    wide_s,
    table_s,
    toeplitz_s,
    turned_s,
    local_s,
    cross_s,
    row_s,
    acc_s,
    own_s,
    in_s,
    out_s,
    got_s,
    own_b,
    in_b,
    out_b,
    got_b,
    norm_own,
    norm_got,
    part_s,
    part_got,
    sum_s,
    sum_got,
    send_sem,
    recv_sem,
    tp_send,
    tp_recv,
    load_sem,
    store_sem,
    part_sem,
):
    here = lax.axis_index("ctx")
    side = lax.axis_index("tp")
    length, channels = gate_ref.shape
    modes, groups = res_ref.shape
    members = channels // groups
    subs = length // SUB
    blocks = channels // LANES
    in_block = LANES // members
    wide = in_block * SUB
    piece_rows = blocks * modes // ctx_count
    per = piece_rows // modes
    shared = (2 * modes) % ctx_count == 0
    part_rows = 2 * modes // ctx_count

    loads = [
        pltpu.make_async_copy(source, target, load_sem.at[k])
        for k, (source, target) in enumerate(
            (
                (res_in, res_ref),
                (log_in, log_ref),
                (key_in, key_ref),
                (value_in, value_ref),
                (skip_in, skip_ref),
                (gate_in, gate_ref),
                (cot_in, cot_ref),
                (gain_in, gain_ref),
            )
        )
    ]
    for load in loads:
        load.start()

    barrier = pltpu.get_barrier_semaphore()
    for d in range(1, ctx_count):
        pl.semaphore_signal(
            barrier, inc=1, device_id={"ctx": lax.rem(here + d, ctx_count)}, device_id_type=MESH
        )
    for d in range(1, tp_count):
        pl.semaphore_signal(
            barrier, inc=1, device_id={"tp": lax.rem(side + d, tp_count)}, device_id_type=MESH
        )

    mask_tok[...] = (
        iota((wide, LANES), 0) // SUB == iota((wide, LANES), 1) // members
    ).astype(F32).astype(BF16)
    mask_mode[...] = (
        iota((in_block * modes, LANES), 0) // modes == iota((in_block * modes, LANES), 1) // members
    ).astype(F32).astype(BF16)
    widen[:, :wide] = (iota((groups, wide), 0) == iota((groups, wide), 1) // SUB).astype(F32).astype(BF16)
    widen[:, wide:] = (
        iota((groups, LANES), 0) == iota((groups, LANES), 1) // members
    ).astype(F32).astype(BF16)
    acc_s[...] = jnp.zeros_like(acc_s)

    def lanes(j, width=LANES):
        return pl.ds(pl.multiple_of(j * width, width), width)

    def stack(value, mask):
        copies = mask.shape[0] // value.shape[0]
        return jnp.concatenate([value] * copies, axis=0) * mask

    def tokens_stack(value):
        mask = mask_tok[...]
        return jnp.concatenate(
            [stack(value[n * SUB : (n + 1) * SUB], mask) for n in range(subs)], axis=1
        )

    def carry_product(table, states):
        mask = mask_mode[...]
        split = [halves(s) for s in states]
        right = [
            jnp.concatenate([stack(s[k], mask) for s in split], axis=1) for k in range(2)
        ]
        out = product(halves(table), right)
        return jnp.concatenate(
            [out[:, n * LANES : (n + 1) * LANES] for n in range(subs)], axis=0
        )

    def put_state(ref, j, value):
        if per:
            ref[j // per, pl.ds(pl.multiple_of((j % per) * modes, modes), modes)] = value
        else:
            count = modes // piece_rows
            for q in range(count):
                ref[j * count + q] = value[q * piece_rows : (q + 1) * piece_rows]

    def take_state(ref, j):
        if per:
            return ref[j // per, pl.ds(pl.multiple_of((j % per) * modes, modes), modes)]
        count = modes // piece_rows
        return jnp.concatenate([ref[j * count + q] for q in range(count)], axis=0)

    def rate_wide(j):
        return wide_s[j, :modes, :wide]

    def res_wide(j):
        return wide_s[j, modes:, :wide]

    def chan_rate(j):
        return wide_s[j, :modes, wide:]

    def signal_of(j):
        at = lanes(j)
        return key_ref[:, at].astype(F32) * value_ref[:, at].astype(F32)

    def strided(row, first):
        parts = []
        for h in range(wide // LANES):
            part = jnp.broadcast_to(row[:, h * LANES : (h + 1) * LANES], (SUB, LANES))
            parts.append(pltpu.roll(part, first, 1, stride=1, stride_axis=0))
        return jnp.concatenate(parts, axis=1)

    def batch(compute, store, js):
        results = [compute(j) for j in js]
        for j, result in zip(js, results):
            store(j, *result)

    def batches(compute, store, first, last, size):
        def step(i, _):
            batch(compute, store, [first + i * size + b for b in range(size)])
            return 0

        lax.fori_loop(0, (last - first) // size, step, 0)

    def transfer(source, target, phase, d, by_target=True):
        there = lax.rem(here + d, ctx_count)
        return pltpu.make_async_remote_copy(
            src_ref=source.at[there] if by_target else source,
            dst_ref=target.at[here],
            send_sem=send_sem.at[phase, d],
            recv_sem=recv_sem.at[phase, d],
            device_id={"ctx": there},
            device_id_type=MESH,
        )

    def all_others(act):
        def step(d, _):
            act(d)
            return 0

        lax.fori_loop(1, ctx_count, step, 0)

    pair = 2 if ctx_count % 2 == 0 else 1

    def piece_blocks(piece):
        return [piece * per + b for b in range(per)]

    def blocks_then_send(compute, store, source, target, phase):
        if per:
            def step(i, _):
                first = i * pair + 1
                batch(
                    compute,
                    store,
                    [
                        j
                        for b in range(pair)
                        for j in piece_blocks(lax.rem(here + first + b, ctx_count))
                    ],
                )
                for b in range(pair):
                    @pl.when(first + b < ctx_count)
                    def _():
                        transfer(source, target, phase, first + b).start()

                return 0

            lax.fori_loop(0, ctx_count // pair, step, 0)
        else:
            batches(compute, store, 0, blocks, 2)
            all_others(lambda d: transfer(source, target, phase, d).start())
        target[here] = source[here]

    def receive_then_blocks(compute, store, source, target, phase):
        target[here] = source[here]
        if per:
            def step(i, _):
                first = i * pair
                for b in range(pair):
                    @pl.when(first + b > 0)
                    def _():
                        transfer(source, target, phase, first + b).wait_recv()

                batch(
                    compute,
                    store,
                    [
                        j
                        for b in range(pair)
                        for j in piece_blocks(lax.rem(here - first - b + ctx_count, ctx_count))
                    ],
                )
                return 0

            lax.fori_loop(0, ctx_count // pair, step, 0)
        else:
            all_others(lambda d: transfer(source, target, phase, d).wait_recv())
            batches(compute, store, 0, blocks, 2)

    def owned_decay():
        if per:
            rates = jnp.concatenate([chan_rate(here * per + b) for b in range(per)], axis=0)
            return jnp.exp(-length * rates)
        count = modes // piece_rows
        whole = chan_rate(here // count)
        rates = whole[:piece_rows]
        for q in range(1, count):
            rates = jnp.where(
                here % count == q, whole[q * piece_rows : (q + 1) * piece_rows], rates
            )
        return jnp.exp(-length * rates)

    def join(own, source, target, result, phase, reverse):
        decay = owned_decay()
        all_others(lambda d: transfer(own, source, phase, d).wait_recv())

        def step(k, state):
            at = ctx_count - 1 - k if reverse else k
            target[at] = state
            return decay * state + source[at]

        lax.fori_loop(0, ctx_count, step, jnp.zeros((piece_rows, LANES), F32), unroll=True)
        all_others(lambda d: transfer(target, result, phase + 1, d).start())

    eye = unit(groups)
    for load in loads[:2]:
        load.wait()
    tables = jnp.concatenate([jnp.exp(log_ref[...]), res_ref[...]], axis=0)
    rates, residues = transposed(tables[:modes], eye), transposed(tables[modes:], eye)
    spread_modes = (
        iota((modes, LANES), 0) == iota((modes, LANES), 1) % modes
    ).astype(F32).astype(BF16)
    own_row = iota((in_block, LANES), 0) == iota((in_block, LANES), 1) // modes
    rolled = [
        pltpu.roll(tables, (groups - j * in_block) % groups, 1) for j in range(blocks)
    ]
    wide_s[...] = ones_dot(jnp.concatenate(rolled, axis=0), widen[...]).reshape(wide_s.shape)
    flat = ones_dot(jnp.concatenate([rates, residues], axis=0), spread_modes)
    for q in range(2):
        for j in range(blocks):
            first = q * groups + j * in_block
            part = jnp.where(own_row, flat[first : first + in_block], 0.0)
            row_s[q, j : j + 1] = jnp.sum(part, axis=0, keepdims=True)

    row_id = iota((SUB, wide), 0)
    lane_id = iota((SUB, wide), 1) % SUB
    offset = (iota((modes, wide), 1) % SUB).astype(F32)
    time = iota((SUB, in_block * modes), 0).astype(F32)

    def states_of(j):
        ending = jnp.exp(-rate_wide(j) * (SUB - offset))
        table = jnp.concatenate([ending, ending * (SUB - offset)], axis=0)
        high, low = halves(signal_of(j))
        out = product(halves(table), (tokens_stack(high), tokens_stack(low)))
        step = jnp.exp(-chan_rate(j) * SUB)
        state = out[:modes, :LANES]
        for n in range(1, subs):
            state = step * state + out[:modes, n * LANES : (n + 1) * LANES]
        return out, state

    def states_put(j, out, state):
        sub_s[j] = out
        put_state(own_s, j, state)

    def local_of(j):
        taps = jnp.sum(
            res_wide(j) * jnp.exp(-rate_wide(j) * (SUB - 1.0 - offset)), axis=0, keepdims=True
        )
        toeplitz = jnp.where(lane_id <= row_id, strided(taps, LANES - SUB + 1), 0.0)
        signal = signal_of(j)
        high, low = halves(signal)
        out = product(halves(toeplitz), (tokens_stack(high), tokens_stack(low)))
        out = jnp.concatenate([out[:, n * LANES : (n + 1) * LANES] for n in range(subs)], axis=0)
        return (out + skip_ref[:, lanes(j)] * signal,)

    def local_put(j, out):
        mixed_s[:, lanes(j)] = out

    def carried_of(j):
        at = lanes(j)
        step = jnp.exp(-chan_rate(j) * SUB)
        state, moment = take_state(got_s, j), jnp.zeros((modes, LANES), F32)
        states, saved = [], []
        for n in range(subs):
            states.append(state)
            saved.append(jnp.concatenate([state, moment], axis=0))
            part = sub_s[j, :, n * LANES : (n + 1) * LANES]
            moment = step * (moment + SUB * state) + part[modes:]
            state = step * state + part[:modes]
        table = row_s[1, pl.ds(j, 1)] * jnp.exp(-row_s[0, pl.ds(j, 1)] * time)
        mixed = mixed_s[:, at] + carry_product(table, states)
        premix = gate_ref[:, at].astype(F32) * mixed
        pull = cot_ref[:, at].astype(F32) * gain_ref[:, at]
        return saved, moment, mixed, premix * premix, pull * premix

    def carried_put(j, saved, moment, mixed, square, inner):
        for n in range(subs):
            state_s[j, n] = saved[n]
        late_s[j] = moment
        mixed_s[:, lanes(j)] = mixed
        acc_s[0] += square
        acc_s[1] += inner

    turn = (iota((SUB, SUB), 0) + iota((SUB, SUB), 1) == SUB - 1).astype(F32).astype(BF16)

    def tables_of(j):
        start = jnp.exp(-rate_wide(j) * offset)
        taps = jnp.sum(res_wide(j) * start, axis=0, keepdims=True)
        toeplitz = jnp.where(lane_id >= row_id, strided(taps, 0), 0.0)
        turned = tuple(
            dot(
                turn,
                jnp.concatenate([part[n * SUB : (n + 1) * SUB] for n in range(subs)], axis=1),
            ).astype(BF16)
            for part in halves(signal_of(j))
        )
        return (
            halves(jnp.concatenate([start, start * offset], axis=0)) + halves(toeplitz) + turned
        )

    def tables_put(j, high, low, toeplitz_high, toeplitz_low, turned_high, turned_low):
        turned_s[j, 0], turned_s[j, 1] = turned_high, turned_low
        table_s[j, 0], table_s[j, 1] = high, low
        toeplitz_s[j, 0], toeplitz_s[j, 1] = toeplitz_high, toeplitz_low

    for load in loads[2:4]:
        load.wait()
    pl.semaphore_wait(barrier, ctx_count - 1 + tp_count - 1)
    half = blocks // 2
    blocks_then_send(states_of, states_put, own_s, in_s, 0)
    loads[4].wait()
    batches(local_of, local_put, 0, half, 4)
    join(own_s, in_s, out_s, got_s, 0, False)
    batches(local_of, local_put, half, blocks, 4)
    batches(tables_of, tables_put, 0, half, 4)
    for load in loads[5:]:
        load.wait()
    receive_then_blocks(carried_of, carried_put, out_s, got_s, 1)

    for k in range(2):
        row = jnp.sum(acc_s[k].T, axis=0, keepdims=True)
        norm_own[4 * k : 4 * k + 4] = jnp.broadcast_to(row, (4, length))
    copies = []
    for d in range(1, tp_count):
        copy = pltpu.make_async_remote_copy(
            src_ref=norm_own,
            dst_ref=norm_got.at[side],
            send_sem=tp_send.at[d],
            recv_sem=tp_recv.at[d],
            device_id={"tp": lax.rem(side + d, tp_count)},
            device_id_type=MESH,
        )
        copy.start()
        copies.append(copy)
    norm_got[side] = norm_own[...]

    batches(tables_of, tables_put, half, blocks, 4)
    for copy in copies:
        copy.wait()
    sums = norm_got[0]
    for k in range(1, tp_count):
        sums = sums + norm_got[k]
    inverse_row = lax.rsqrt(sums[0:1] / full_width + EPSILON)
    inner_row = sums[4:5] * inverse_row / full_width
    acc_s[0] = jnp.broadcast_to(inverse_row, (LANES, length)).T
    acc_s[1] = jnp.broadcast_to(inner_row, (LANES, length)).T

    to_group = (
        iota((LANES, groups), 0) // members == iota((LANES, groups), 1)
    ).astype(F32).astype(BF16)
    wide_to_group = (
        iota((wide, groups), 0) // SUB == iota((wide, groups), 1)
    ).astype(F32).astype(BF16)

    def weight_of(j):
        at = lanes(j)
        inverse, inner = acc_s[0], acc_s[1]
        gate = gate_ref[:, at].astype(F32)
        normed = gate * mixed_s[:, at] * inverse
        dpre = (cot_ref[:, at].astype(F32) * gain_ref[:, at] - normed * inner) * inverse
        weight = dpre * gate
        high, low = halves(weight)
        out = product((table_s[j, 0], table_s[j, 1]), (tokens_stack(high), tokens_stack(low)))
        step = jnp.exp(-chan_rate(j) * SUB)
        state = out[:modes, (subs - 1) * LANES :]
        for n in range(subs - 2, -1, -1):
            state = step * state + out[:modes, n * LANES : (n + 1) * LANES]
        return weight, out, state

    def weight_put(j, weight, out, state):
        weight_s[:, lanes(j)] = weight
        sub_s[j] = out
        put_state(own_b, j, state)

    def inside_of(j):
        at = lanes(j)
        inverse, inner = acc_s[0], acc_s[1]
        mixed = mixed_s[:, at]
        gain = gain_ref[:, at]
        normed = gate_ref[:, at].astype(F32) * mixed * inverse
        dpre = (cot_ref[:, at].astype(F32) * gain - normed * inner) * inverse
        weight = weight_s[:, at]
        start = jnp.exp(-rate_wide(j) * offset)
        high, low = halves(weight)
        right = (tokens_stack(high), tokens_stack(low))
        back = product((toeplitz_s[j, 0], toeplitz_s[j, 1]), right)
        back = jnp.concatenate([back[:, n * LANES : (n + 1) * LANES] for n in range(subs)], axis=0)

        pairs = product((turned_s[j, 0], turned_s[j, 1]), right, dot_t)
        pairs = jnp.where(lane_id + row_id >= SUB - 1, pairs, 0.0)
        lagged = [
            jnp.sum(
                pltpu.roll(
                    pairs[:, h * LANES : (h + 1) * LANES], LANES - SUB + 1, 1, stride=1, stride_axis=0
                ),
                axis=0,
                keepdims=True,
            )
            for h in range(wide // LANES)
        ]
        zeroth = start * jnp.concatenate(lagged, axis=1)
        local = jnp.concatenate([zeroth, zeroth * offset], axis=0)

        cross = jnp.zeros((modes, LANES), F32)
        cross_moment = jnp.zeros((modes, LANES), F32)
        for n in range(subs):
            part = sub_s[j, :, n * LANES : (n + 1) * LANES]
            both = state_s[j, n]
            cross += part[:modes] * both[:modes]
            cross_moment += part[modes:] * both[:modes] + part[:modes] * both[modes:]
        return (
            (normed * gain).astype(BF16),
            (dpre * mixed).astype(BF16),
            back + skip_ref[:, at] * weight,
            local,
            jnp.concatenate([cross, cross_moment], axis=0),
        )

    def inside_put(j, mixer, grad_q, back, local, cross):
        at = lanes(j)
        mixer_ref[:, at] = mixer
        gq_ref[:, at] = grad_q
        back_s[:, at] = back
        local_s[j] = local
        cross_s[j] = cross

    def ending_of(j):
        return (cross_s[j, modes:] + take_state(got_b, j) * late_s[j],)

    def ending_put(j, moment):
        cross_s[j, modes:] = moment

    def group_sums(ref, ones):
        rows = ones_dot(ref[...].reshape(blocks * 2 * modes, ref.shape[2]), ones)
        total = rows[: 2 * modes]
        for j in range(1, blocks):
            total += pltpu.roll(rows[2 * modes * j : 2 * modes * (j + 1)], j * in_block, 1)
        return total

    def signal_grad_of(j):
        at = lanes(j)
        step = jnp.exp(-chan_rate(j) * SUB)
        state = take_state(got_b, j)
        states = []
        for n in range(subs - 1, -1, -1):
            states.append(state)
            state = step * state + sub_s[j, :modes, n * LANES : (n + 1) * LANES]
        states.reverse()
        table = row_s[1, pl.ds(j, 1)] * jnp.exp(-row_s[0, pl.ds(j, 1)] * (SUB - time))
        grad = back_s[:, at] + carry_product(table, states)
        return (
            (grad * value_ref[:, at].astype(F32)).astype(BF16),
            (grad * key_ref[:, at].astype(F32)).astype(BF16),
        )

    def signal_grad_put(j, grad_k, grad_v):
        gk_ref[:, lanes(j)] = grad_k
        gv_ref[:, lanes(j)] = grad_v

    blocks_then_send(weight_of, weight_put, own_b, in_b, 2)
    batches(inside_of, inside_put, 0, half, 4)
    join(own_b, in_b, out_b, got_b, 2, True)
    batches(inside_of, inside_put, half, blocks, 4)
    stores = [
        pltpu.make_async_copy(mixer_ref, mixer_out, store_sem.at[0]),
        pltpu.make_async_copy(gq_ref, gq_out, store_sem.at[1]),
    ]
    for store in stores:
        store.start()
    inside_total = group_sums(local_s, wide_to_group)
    receive_then_blocks(ending_of, ending_put, out_b, got_b, 3)
    total = inside_total + group_sums(cross_s, to_group)
    if shared:
        for k in range(ctx_count):
            part_s[k] = total[k * part_rows : (k + 1) * part_rows]
        all_others(lambda d: transfer(part_s, part_got, 4, d).start())
        part_got[here] = part_s[here]
    else:
        part_s[...] = total
        all_others(lambda d: transfer(part_s, part_got, 4, d, False).start())
        part_got[here] = part_s[...]

    size = 4

    def grad_stores(i):
        at = lanes(i, size * LANES)
        return [
            pltpu.make_async_copy(source.at[:, at], target.at[:, at], part_sem.at[k, i])
            for k, (source, target) in enumerate(((gk_ref, gk_out), (gv_ref, gv_out)))
        ]

    def grads(i, _):
        batch(signal_grad_of, signal_grad_put, [i * size + b for b in range(size)])
        for store in grad_stores(i):
            store.start()
        return 0

    lax.fori_loop(0, blocks // size // 2, grads, 0)
    all_others(lambda d: transfer(part_s, part_got, 4, d, shared).wait_recv())
    sums = part_got[0]
    for k in range(1, ctx_count):
        sums = sums + part_got[k]
    if shared:
        sum_s[...] = sums
        all_others(lambda d: transfer(sum_s, sum_got, 5, d, False).start())
        sum_got[here] = sums
    lax.fori_loop(blocks // size // 2, blocks // size, grads, 0)
    if shared:
        all_others(lambda d: transfer(sum_s, sum_got, 5, d, False).wait())
        sums = jnp.concatenate([sum_got[k] for k in range(ctx_count)], axis=0)
    scale = 1.0 / (length * ctx_count)
    filt_ref[:modes] = sums[:modes] * scale
    filt_ref[modes:] = -res_ref[...] * jnp.exp(log_ref[...]) * sums[modes:] * scale
    last = [
        pltpu.make_async_copy(filt_ref.at[:modes], res_out, store_sem.at[2]),
        pltpu.make_async_copy(filt_ref.at[modes:], log_out, store_sem.at[3]),
    ]
    for store in last:
        store.start()

    def drain(d):
        transfer(part_s, part_got, 4, d, shared).wait_send()
        for phase, (source, target) in enumerate(
            ((own_s, in_s), (out_s, got_s), (own_b, in_b), (out_b, got_b))
        ):
            transfer(source, target, phase, d).wait_send()

    all_others(drain)
    for i in range(blocks // size):
        stores += grad_stores(i)
    for store in stores + last:
        store.wait()


def finish(*refs):
    sources, targets, held, (load_sem, store_sem) = refs[:6], refs[6:12], refs[12:18], refs[18:]
    loads, stores = [], []
    for k, (source, target, middle) in enumerate(zip(sources, targets, held)):
        rows = min(source.shape[0], PART_ROWS)
        for q in range(source.shape[0] // rows):
            at = pl.ds(q * rows, rows)
            loads.append(pltpu.make_async_copy(source.at[at], middle.at[at], load_sem.at[k, q]))
            stores.append(pltpu.make_async_copy(middle.at[at], target.at[at], store_sem.at[k, q]))
    for load in loads:
        load.start()
    for load, store in zip(loads, stores):
        load.wait()
        store.start()
    for store in stores:
        store.wait()


def per_device(out_gate, key_proj, value_proj, residue, log_decay, skip, gain, cotangent):
    length, channels = out_gate.shape
    groups, modes = residue.shape
    members = channels // groups
    ctx_count, tp_count = lax.axis_size("ctx"), lax.axis_size("tp")
    blocks = channels // LANES
    in_block = LANES // members
    subs = length // SUB
    wide = in_block * SUB
    piece_rows = blocks * modes // ctx_count
    part_shape = (2 * modes, groups)
    if (2 * modes) % ctx_count == 0:
        part_shape = (ctx_count, 2 * modes // ctx_count, groups)
    pieces = pltpu.VMEM((ctx_count, piece_rows, LANES), F32)
    wide_out = jax.ShapeDtypeStruct((length, channels), BF16)
    table_out = jax.ShapeDtypeStruct((modes, groups), F32)
    hbm = pl.BlockSpec(memory_space=pltpu.HBM)
    results = [wide_out] * 4 + [table_out] * 2
    computed = pl.pallas_call(
        functools.partial(kernel, ctx_count, tp_count, float(channels * tp_count)),
        out_shape=results,
        in_specs=[hbm] * 8,
        out_specs=[hbm] * 6,
        scratch_shapes=[
            pltpu.VMEM((length, channels), BF16),
            pltpu.VMEM((length, channels), BF16),
            pltpu.VMEM((length, channels), BF16),
            pltpu.VMEM((length, channels), BF16),
            pltpu.VMEM((1, channels), F32),
            pltpu.VMEM((1, channels), F32),
            pltpu.VMEM((modes, groups), F32),
            pltpu.VMEM((modes, groups), F32),
            pltpu.VMEM((length, channels), BF16),
            pltpu.VMEM((length, channels), BF16),
            pltpu.VMEM((length, channels), BF16),
            pltpu.VMEM((length, channels), BF16),
            pltpu.VMEM((2 * modes, groups), F32),
            pltpu.VMEM((length, channels), F32),
            pltpu.VMEM((length, channels), F32),
            pltpu.VMEM((length, channels), F32),
            pltpu.VMEM((blocks, 2 * modes, subs * LANES), F32),
            pltpu.VMEM((blocks, subs, 2 * modes, LANES), F32),
            pltpu.VMEM((blocks, modes, LANES), F32),
            pltpu.VMEM((wide, LANES), BF16),
            pltpu.VMEM((in_block * modes, LANES), BF16),
            pltpu.VMEM((groups, wide + LANES), BF16),
            pltpu.VMEM((blocks, 2 * modes, wide + LANES), F32),
            pltpu.VMEM((blocks, 2, 2 * modes, wide), BF16),
            pltpu.VMEM((blocks, 2, SUB, wide), BF16),
            pltpu.VMEM((blocks, 2, SUB, subs * LANES), BF16),
            pltpu.VMEM((blocks, 2 * modes, wide), F32),
            pltpu.VMEM((blocks, 2 * modes, LANES), F32),
            pltpu.VMEM((2, blocks, LANES), F32),
            pltpu.VMEM((2, length, LANES), F32),
            pieces, pieces, pieces, pieces,
            pieces, pieces, pieces, pieces,
            pltpu.VMEM((8, length), F32),
            pltpu.VMEM((tp_count, 8, length), F32),
            pltpu.VMEM(part_shape, F32),
            pltpu.VMEM((ctx_count,) + part_shape[-2:], F32),
            pltpu.VMEM(part_shape[-2:], F32),
            pltpu.VMEM((ctx_count,) + part_shape[-2:], F32),
            pltpu.SemaphoreType.DMA((6, ctx_count)),
            pltpu.SemaphoreType.DMA((6, ctx_count)),
            pltpu.SemaphoreType.DMA((tp_count,)),
            pltpu.SemaphoreType.DMA((tp_count,)),
            pltpu.SemaphoreType.DMA((8,)),
            pltpu.SemaphoreType.DMA((4,)),
            pltpu.SemaphoreType.DMA((2, blocks)),
        ],
        compiler_params=pltpu.CompilerParams(
            collective_id=0, has_side_effects=True, vmem_limit_bytes=60 * 1024 * 1024
        ),
        name="mixer",
    )(out_gate, key_proj, value_proj, cotangent, skip[None], gain[None], residue.T, log_decay.T)
    *wide_results, grad_residue, grad_log_decay = pl.pallas_call(
        finish,
        out_shape=results,
        in_specs=[hbm] * 6,
        out_specs=[hbm] * 6,
        scratch_shapes=[pltpu.VMEM(result.shape, result.dtype) for result in results]
        + [pltpu.SemaphoreType.DMA((6, length // PART_ROWS))] * 2,
        compiler_params=pltpu.CompilerParams(vmem_limit_bytes=60 * 1024 * 1024),
        name="finish",
    )(*computed)
    return *wide_results, grad_residue.T, grad_log_decay.T


def solution(mesh):
    wide, table, row = P("ctx", "tp"), P("tp", None), P("tp")
    return jax.shard_map(
        per_device,
        mesh=mesh,
        in_specs=(wide, wide, wide, table, table, row, row, wide),
        out_specs=(wide, wide, wide, wide, table, table),
        check_vma=False,
    )
```

```python
import functools

import jax
import jax.numpy as jnp
from jax import lax
from jax.experimental import pallas as pl
from jax.experimental.pallas import tpu as pltpu
from jax.sharding import PartitionSpec as P

EPSILON = 1e-06
LANES = 128
SUB = 32
PART_ROWS = 64
F32 = jnp.float32
BF16 = jnp.bfloat16
MESH = pl.DeviceIdType.MESH


def halves(value):
    high = value.astype(BF16)
    return high, (value - high.astype(F32)).astype(BF16)


def dot(a, b):
    return jnp.dot(a, b, preferred_element_type=F32)


def dot_t(a, b):
    return lax.dot_general(a, b, (((1,), (1,)), ((), ())), preferred_element_type=F32)


def product(left, right, multiply=dot):
    rows = left[0].shape[0]
    both = multiply(jnp.concatenate(left, axis=0), right[0])
    return both[:rows] + both[rows:] + multiply(left[0], right[1])


def ones_dot(value, ones):
    rows = value.shape[0]
    out = dot(jnp.concatenate(halves(value), axis=0), ones)
    return out[:rows] + out[rows:]


def iota(shape, dim):
    return lax.broadcasted_iota(jnp.int32, shape, dim)


def transposed(value, eye):
    high = value.astype(BF16)
    rest = value - high.astype(F32)
    mid = rest.astype(BF16)
    low = (rest - mid.astype(F32)).astype(BF16)
    return dot_t(eye, high) + dot_t(eye, mid) + dot_t(eye, low)


def unit(size):
    return (iota((size, size), 0) == iota((size, size), 1)).astype(F32).astype(BF16)


def kernel(
    ctx_count,
    tp_count,
    full_width,
    gate_in,
    key_in,
    value_in,
    cot_in,
    skip_in,
    gain_in,
    res_in,
    log_in,
    mixer_out,
    gq_out,
    gk_out,
    gv_out,
    res_out,
    log_out,
    gate_ref,
    key_ref,
    value_ref,
    cot_ref,
    skip_ref,
    gain_ref,
    res_ref,
    log_ref,
    mixer_ref,
    gq_ref,
    gk_ref,
    gv_ref,
    filt_ref,
    mixed_s,
    weight_s,
    back_s,
    sub_s,
    state_s,
    late_s,
    mask_tok,
    mask_mode,
    widen,
    wide_s,
    table_s,
    toeplitz_s,
    turned_s,
    local_s,
    cross_s,
    row_s,
    acc_s,
    own_s,
    in_s,
    out_s,
    got_s,
    own_b,
    in_b,
    out_b,
    got_b,
    norm_own,
    norm_got,
    part_s,
    part_got,
    send_sem,
    recv_sem,
    tp_send,
    tp_recv,
    load_sem,
    store_sem,
    part_sem,
):
    here = lax.axis_index("ctx")
    side = lax.axis_index("tp")
    length, channels = gate_ref.shape
    modes, groups = res_ref.shape
    members = channels // groups
    subs = length // SUB
    blocks = channels // LANES
    in_block = LANES // members
    wide = in_block * SUB
    piece_rows = blocks * modes // ctx_count
    per = piece_rows // modes

    loads = [
        pltpu.make_async_copy(source, target, load_sem.at[k])
        for k, (source, target) in enumerate(
            (
                (res_in, res_ref),
                (log_in, log_ref),
                (key_in, key_ref),
                (value_in, value_ref),
                (skip_in, skip_ref),
                (gate_in, gate_ref),
                (cot_in, cot_ref),
                (gain_in, gain_ref),
            )
        )
    ]
    for load in loads:
        load.start()

    barrier = pltpu.get_barrier_semaphore()
    for d in range(1, ctx_count):
        pl.semaphore_signal(
            barrier, inc=1, device_id={"ctx": lax.rem(here + d, ctx_count)}, device_id_type=MESH
        )
    for d in range(1, tp_count):
        pl.semaphore_signal(
            barrier, inc=1, device_id={"tp": lax.rem(side + d, tp_count)}, device_id_type=MESH
        )

    mask_tok[...] = (
        iota((wide, LANES), 0) // SUB == iota((wide, LANES), 1) // members
    ).astype(F32).astype(BF16)
    mask_mode[...] = (
        iota((in_block * modes, LANES), 0) // modes == iota((in_block * modes, LANES), 1) // members
    ).astype(F32).astype(BF16)
    widen[:, :wide] = (iota((groups, wide), 0) == iota((groups, wide), 1) // SUB).astype(F32).astype(BF16)
    widen[:, wide:] = (
        iota((groups, LANES), 0) == iota((groups, LANES), 1) // members
    ).astype(F32).astype(BF16)
    acc_s[...] = jnp.zeros_like(acc_s)

    def lanes(j, width=LANES):
        return pl.ds(pl.multiple_of(j * width, width), width)

    def stack(value, mask):
        copies = mask.shape[0] // value.shape[0]
        return jnp.concatenate([value] * copies, axis=0) * mask

    def tokens_stack(value):
        mask = mask_tok[...]
        return jnp.concatenate(
            [stack(value[n * SUB : (n + 1) * SUB], mask) for n in range(subs)], axis=1
        )

    def carry_product(table, states):
        mask = mask_mode[...]
        split = [halves(s) for s in states]
        right = [
            jnp.concatenate([stack(s[k], mask) for s in split], axis=1) for k in range(2)
        ]
        out = product(halves(table), right)
        return jnp.concatenate(
            [out[:, n * LANES : (n + 1) * LANES] for n in range(subs)], axis=0
        )

    def put_state(ref, j, value):
        if per:
            ref[j // per, pl.ds(pl.multiple_of((j % per) * modes, modes), modes)] = value
        else:
            count = modes // piece_rows
            for q in range(count):
                ref[j * count + q] = value[q * piece_rows : (q + 1) * piece_rows]

    def take_state(ref, j):
        if per:
            return ref[j // per, pl.ds(pl.multiple_of((j % per) * modes, modes), modes)]
        count = modes // piece_rows
        return jnp.concatenate([ref[j * count + q] for q in range(count)], axis=0)

    def rate_wide(j):
        return wide_s[j, :modes, :wide]

    def res_wide(j):
        return wide_s[j, modes:, :wide]

    def chan_rate(j):
        return wide_s[j, :modes, wide:]

    def signal_of(j):
        at = lanes(j)
        return key_ref[:, at].astype(F32) * value_ref[:, at].astype(F32)

    def strided(row, first):
        parts = []
        for h in range(wide // LANES):
            part = jnp.broadcast_to(row[:, h * LANES : (h + 1) * LANES], (SUB, LANES))
            parts.append(pltpu.roll(part, first, 1, stride=1, stride_axis=0))
        return jnp.concatenate(parts, axis=1)

    def batch(compute, store, js):
        results = [compute(j) for j in js]
        for j, result in zip(js, results):
            store(j, *result)

    def batches(compute, store, first, last, size):
        def step(i, _):
            batch(compute, store, [first + i * size + b for b in range(size)])
            return 0

        lax.fori_loop(0, (last - first) // size, step, 0)

    def transfer(source, target, phase, d, by_target=True):
        there = lax.rem(here + d, ctx_count)
        return pltpu.make_async_remote_copy(
            src_ref=source.at[there] if by_target else source,
            dst_ref=target.at[here],
            send_sem=send_sem.at[phase, d],
            recv_sem=recv_sem.at[phase, d],
            device_id={"ctx": there},
            device_id_type=MESH,
        )

    def all_others(act):
        def step(d, _):
            act(d)
            return 0

        lax.fori_loop(1, ctx_count, step, 0)

    pair = 2 if ctx_count % 2 == 0 else 1

    def piece_blocks(piece):
        return [piece * per + b for b in range(per)]

    def blocks_then_send(compute, store, source, target, phase):
        if per:
            def step(i, _):
                first = i * pair + 1
                batch(
                    compute,
                    store,
                    [
                        j
                        for b in range(pair)
                        for j in piece_blocks(lax.rem(here + first + b, ctx_count))
                    ],
                )
                for b in range(pair):
                    @pl.when(first + b < ctx_count)
                    def _():
                        transfer(source, target, phase, first + b).start()

                return 0

            lax.fori_loop(0, ctx_count // pair, step, 0)
        else:
            batches(compute, store, 0, blocks, 2)
            all_others(lambda d: transfer(source, target, phase, d).start())
        target[here] = source[here]

    def receive_then_blocks(compute, store, source, target, phase):
        target[here] = source[here]
        if per:
            def step(i, _):
                first = i * pair
                for b in range(pair):
                    @pl.when(first + b > 0)
                    def _():
                        transfer(source, target, phase, first + b).wait_recv()

                batch(
                    compute,
                    store,
                    [
                        j
                        for b in range(pair)
                        for j in piece_blocks(lax.rem(here - first - b + ctx_count, ctx_count))
                    ],
                )
                return 0

            lax.fori_loop(0, ctx_count // pair, step, 0)
        else:
            all_others(lambda d: transfer(source, target, phase, d).wait_recv())
            batches(compute, store, 0, blocks, 2)

    def owned_decay():
        if per:
            rates = jnp.concatenate([chan_rate(here * per + b) for b in range(per)], axis=0)
            return jnp.exp(-length * rates)
        count = modes // piece_rows
        whole = chan_rate(here // count)
        rates = whole[:piece_rows]
        for q in range(1, count):
            rates = jnp.where(
                here % count == q, whole[q * piece_rows : (q + 1) * piece_rows], rates
            )
        return jnp.exp(-length * rates)

    def join(own, source, target, result, phase, reverse):
        decay = owned_decay()
        all_others(lambda d: transfer(own, source, phase, d).wait_recv())

        def step(k, state):
            at = ctx_count - 1 - k if reverse else k
            target[at] = state
            return decay * state + source[at]

        lax.fori_loop(0, ctx_count, step, jnp.zeros((piece_rows, LANES), F32), unroll=True)
        all_others(lambda d: transfer(target, result, phase + 1, d).start())

    eye = unit(groups)
    for load in loads[:2]:
        load.wait()
    tables = jnp.concatenate([jnp.exp(log_ref[...]), res_ref[...]], axis=0)
    rates, residues = transposed(tables[:modes], eye), transposed(tables[modes:], eye)
    spread_modes = (
        iota((modes, LANES), 0) == iota((modes, LANES), 1) % modes
    ).astype(F32).astype(BF16)
    own_row = iota((in_block, LANES), 0) == iota((in_block, LANES), 1) // modes
    rolled = [
        pltpu.roll(tables, (groups - j * in_block) % groups, 1) for j in range(blocks)
    ]
    wide_s[...] = ones_dot(jnp.concatenate(rolled, axis=0), widen[...]).reshape(wide_s.shape)
    flat = ones_dot(jnp.concatenate([rates, residues], axis=0), spread_modes)
    for q in range(2):
        for j in range(blocks):
            first = q * groups + j * in_block
            part = jnp.where(own_row, flat[first : first + in_block], 0.0)
            row_s[q, j : j + 1] = jnp.sum(part, axis=0, keepdims=True)

    row_id = iota((SUB, wide), 0)
    lane_id = iota((SUB, wide), 1) % SUB
    offset = (iota((modes, wide), 1) % SUB).astype(F32)
    time = iota((SUB, in_block * modes), 0).astype(F32)

    def states_of(j):
        ending = jnp.exp(-rate_wide(j) * (SUB - offset))
        table = jnp.concatenate([ending, ending * (SUB - offset)], axis=0)
        high, low = halves(signal_of(j))
        out = product(halves(table), (tokens_stack(high), tokens_stack(low)))
        step = jnp.exp(-chan_rate(j) * SUB)
        state = out[:modes, :LANES]
        for n in range(1, subs):
            state = step * state + out[:modes, n * LANES : (n + 1) * LANES]
        return out, state

    def states_put(j, out, state):
        sub_s[j] = out
        put_state(own_s, j, state)

    def local_of(j):
        taps = jnp.sum(
            res_wide(j) * jnp.exp(-rate_wide(j) * (SUB - 1.0 - offset)), axis=0, keepdims=True
        )
        toeplitz = jnp.where(lane_id <= row_id, strided(taps, LANES - SUB + 1), 0.0)
        signal = signal_of(j)
        high, low = halves(signal)
        out = product(halves(toeplitz), (tokens_stack(high), tokens_stack(low)))
        out = jnp.concatenate([out[:, n * LANES : (n + 1) * LANES] for n in range(subs)], axis=0)
        return (out + skip_ref[:, lanes(j)] * signal,)

    def local_put(j, out):
        mixed_s[:, lanes(j)] = out

    def carried_of(j):
        at = lanes(j)
        step = jnp.exp(-chan_rate(j) * SUB)
        state, moment = take_state(got_s, j), jnp.zeros((modes, LANES), F32)
        states, saved = [], []
        for n in range(subs):
            states.append(state)
            saved.append(jnp.concatenate([state, moment], axis=0))
            part = sub_s[j, :, n * LANES : (n + 1) * LANES]
            moment = step * (moment + SUB * state) + part[modes:]
            state = step * state + part[:modes]
        table = row_s[1, pl.ds(j, 1)] * jnp.exp(-row_s[0, pl.ds(j, 1)] * time)
        mixed = mixed_s[:, at] + carry_product(table, states)
        premix = gate_ref[:, at].astype(F32) * mixed
        pull = cot_ref[:, at].astype(F32) * gain_ref[:, at]
        return saved, moment, mixed, premix * premix, pull * premix

    def carried_put(j, saved, moment, mixed, square, inner):
        for n in range(subs):
            state_s[j, n] = saved[n]
        late_s[j] = moment
        mixed_s[:, lanes(j)] = mixed
        acc_s[0] += square
        acc_s[1] += inner

    for load in loads[2:4]:
        load.wait()
    pl.semaphore_wait(barrier, ctx_count - 1 + tp_count - 1)
    half = blocks // 2
    blocks_then_send(states_of, states_put, own_s, in_s, 0)
    loads[4].wait()
    batches(local_of, local_put, 0, half, 4)
    join(own_s, in_s, out_s, got_s, 0, False)
    batches(local_of, local_put, half, blocks, 4)
    for load in loads[5:]:
        load.wait()
    receive_then_blocks(carried_of, carried_put, out_s, got_s, 1)

    for k in range(2):
        row = jnp.sum(acc_s[k].T, axis=0, keepdims=True)
        norm_own[4 * k : 4 * k + 4] = jnp.broadcast_to(row, (4, length))
    copies = []
    for d in range(1, tp_count):
        copy = pltpu.make_async_remote_copy(
            src_ref=norm_own,
            dst_ref=norm_got.at[side],
            send_sem=tp_send.at[d],
            recv_sem=tp_recv.at[d],
            device_id={"tp": lax.rem(side + d, tp_count)},
            device_id_type=MESH,
        )
        copy.start()
        copies.append(copy)
    norm_got[side] = norm_own[...]

    turn = (iota((SUB, SUB), 0) + iota((SUB, SUB), 1) == SUB - 1).astype(F32).astype(BF16)

    def tables_of(j):
        start = jnp.exp(-rate_wide(j) * offset)
        taps = jnp.sum(res_wide(j) * start, axis=0, keepdims=True)
        toeplitz = jnp.where(lane_id >= row_id, strided(taps, 0), 0.0)
        turned = tuple(
            dot(
                turn,
                jnp.concatenate([part[n * SUB : (n + 1) * SUB] for n in range(subs)], axis=1),
            ).astype(BF16)
            for part in halves(signal_of(j))
        )
        return (
            halves(jnp.concatenate([start, start * offset], axis=0)) + halves(toeplitz) + turned
        )

    def tables_put(j, high, low, toeplitz_high, toeplitz_low, turned_high, turned_low):
        turned_s[j, 0], turned_s[j, 1] = turned_high, turned_low
        table_s[j, 0], table_s[j, 1] = high, low
        toeplitz_s[j, 0], toeplitz_s[j, 1] = toeplitz_high, toeplitz_low

    batches(tables_of, tables_put, 0, blocks, 4)
    for copy in copies:
        copy.wait()
    sums = norm_got[0]
    for k in range(1, tp_count):
        sums = sums + norm_got[k]
    inverse_row = lax.rsqrt(sums[0:1] / full_width + EPSILON)
    inner_row = sums[4:5] * inverse_row / full_width
    acc_s[0] = jnp.broadcast_to(inverse_row, (LANES, length)).T
    acc_s[1] = jnp.broadcast_to(inner_row, (LANES, length)).T

    to_group = (
        iota((LANES, groups), 0) // members == iota((LANES, groups), 1)
    ).astype(F32).astype(BF16)
    wide_to_group = (
        iota((wide, groups), 0) // SUB == iota((wide, groups), 1)
    ).astype(F32).astype(BF16)

    def weight_of(j):
        at = lanes(j)
        inverse, inner = acc_s[0], acc_s[1]
        gate = gate_ref[:, at].astype(F32)
        normed = gate * mixed_s[:, at] * inverse
        dpre = (cot_ref[:, at].astype(F32) * gain_ref[:, at] - normed * inner) * inverse
        weight = dpre * gate
        high, low = halves(weight)
        out = product((table_s[j, 0], table_s[j, 1]), (tokens_stack(high), tokens_stack(low)))
        step = jnp.exp(-chan_rate(j) * SUB)
        state = out[:modes, (subs - 1) * LANES :]
        for n in range(subs - 2, -1, -1):
            state = step * state + out[:modes, n * LANES : (n + 1) * LANES]
        return weight, out, state

    def weight_put(j, weight, out, state):
        weight_s[:, lanes(j)] = weight
        sub_s[j] = out
        put_state(own_b, j, state)

    def inside_of(j):
        at = lanes(j)
        inverse, inner = acc_s[0], acc_s[1]
        mixed = mixed_s[:, at]
        gain = gain_ref[:, at]
        normed = gate_ref[:, at].astype(F32) * mixed * inverse
        dpre = (cot_ref[:, at].astype(F32) * gain - normed * inner) * inverse
        weight = weight_s[:, at]
        start = jnp.exp(-rate_wide(j) * offset)
        high, low = halves(weight)
        right = (tokens_stack(high), tokens_stack(low))
        back = product((toeplitz_s[j, 0], toeplitz_s[j, 1]), right)
        back = jnp.concatenate([back[:, n * LANES : (n + 1) * LANES] for n in range(subs)], axis=0)

        pairs = product((turned_s[j, 0], turned_s[j, 1]), right, dot_t)
        pairs = jnp.where(lane_id + row_id >= SUB - 1, pairs, 0.0)
        lagged = [
            jnp.sum(
                pltpu.roll(
                    pairs[:, h * LANES : (h + 1) * LANES], LANES - SUB + 1, 1, stride=1, stride_axis=0
                ),
                axis=0,
                keepdims=True,
            )
            for h in range(wide // LANES)
        ]
        zeroth = start * jnp.concatenate(lagged, axis=1)
        local = jnp.concatenate([zeroth, zeroth * offset], axis=0)

        cross = jnp.zeros((modes, LANES), F32)
        cross_moment = jnp.zeros((modes, LANES), F32)
        for n in range(subs):
            part = sub_s[j, :, n * LANES : (n + 1) * LANES]
            both = state_s[j, n]
            cross += part[:modes] * both[:modes]
            cross_moment += part[modes:] * both[:modes] + part[:modes] * both[modes:]
        return (
            (normed * gain).astype(BF16),
            (dpre * mixed).astype(BF16),
            back + skip_ref[:, at] * weight,
            local,
            jnp.concatenate([cross, cross_moment], axis=0),
        )

    def inside_put(j, mixer, grad_q, back, local, cross):
        at = lanes(j)
        mixer_ref[:, at] = mixer
        gq_ref[:, at] = grad_q
        back_s[:, at] = back
        local_s[j] = local
        cross_s[j] = cross

    def ending_of(j):
        return (cross_s[j, modes:] + take_state(got_b, j) * late_s[j],)

    def ending_put(j, moment):
        cross_s[j, modes:] = moment

    def group_sums(ref, ones):
        rows = ones_dot(ref[...].reshape(blocks * 2 * modes, ref.shape[2]), ones)
        total = rows[: 2 * modes]
        for j in range(1, blocks):
            total += pltpu.roll(rows[2 * modes * j : 2 * modes * (j + 1)], j * in_block, 1)
        return total

    def signal_grad_of(j):
        at = lanes(j)
        step = jnp.exp(-chan_rate(j) * SUB)
        state = take_state(got_b, j)
        states = []
        for n in range(subs - 1, -1, -1):
            states.append(state)
            state = step * state + sub_s[j, :modes, n * LANES : (n + 1) * LANES]
        states.reverse()
        table = row_s[1, pl.ds(j, 1)] * jnp.exp(-row_s[0, pl.ds(j, 1)] * (SUB - time))
        grad = back_s[:, at] + carry_product(table, states)
        return (
            (grad * value_ref[:, at].astype(F32)).astype(BF16),
            (grad * key_ref[:, at].astype(F32)).astype(BF16),
        )

    def signal_grad_put(j, grad_k, grad_v):
        gk_ref[:, lanes(j)] = grad_k
        gv_ref[:, lanes(j)] = grad_v

    blocks_then_send(weight_of, weight_put, own_b, in_b, 2)
    batches(inside_of, inside_put, 0, half, 4)
    join(own_b, in_b, out_b, got_b, 2, True)
    batches(inside_of, inside_put, half, blocks, 4)
    stores = [
        pltpu.make_async_copy(mixer_ref, mixer_out, store_sem.at[0]),
        pltpu.make_async_copy(gq_ref, gq_out, store_sem.at[1]),
    ]
    for store in stores:
        store.start()
    inside_total = group_sums(local_s, wide_to_group)
    receive_then_blocks(ending_of, ending_put, out_b, got_b, 3)
    part_s[...] = inside_total + group_sums(cross_s, to_group)
    all_others(lambda d: transfer(part_s, part_got, 4, d, False).start())
    part_got[here] = part_s[...]

    size = 4

    def grad_stores(i):
        at = lanes(i, size * LANES)
        return [
            pltpu.make_async_copy(source.at[:, at], target.at[:, at], part_sem.at[k, i])
            for k, (source, target) in enumerate(((gk_ref, gk_out), (gv_ref, gv_out)))
        ]

    def grads(i, _):
        batch(signal_grad_of, signal_grad_put, [i * size + b for b in range(size)])
        for store in grad_stores(i):
            store.start()
        return 0

    lax.fori_loop(0, blocks // size, grads, 0)
    all_others(lambda d: transfer(part_s, part_got, 4, d, False).wait())
    sums = part_got[0]
    for k in range(1, ctx_count):
        sums = sums + part_got[k]
    scale = 1.0 / (length * ctx_count)
    filt_ref[:modes] = sums[:modes] * scale
    filt_ref[modes:] = -res_ref[...] * jnp.exp(log_ref[...]) * sums[modes:] * scale
    last = [
        pltpu.make_async_copy(filt_ref.at[:modes], res_out, store_sem.at[2]),
        pltpu.make_async_copy(filt_ref.at[modes:], log_out, store_sem.at[3]),
    ]
    for store in last:
        store.start()

    def drain(d):
        for phase, (source, target) in enumerate(
            ((own_s, in_s), (out_s, got_s), (own_b, in_b), (out_b, got_b))
        ):
            transfer(source, target, phase, d).wait_send()

    all_others(drain)
    for i in range(blocks // size):
        stores += grad_stores(i)
    for store in stores + last:
        store.wait()


def finish(*refs):
    sources, targets, held, (load_sem, store_sem) = refs[:6], refs[6:12], refs[12:18], refs[18:]
    loads, stores = [], []
    for k, (source, target, middle) in enumerate(zip(sources, targets, held)):
        rows = min(source.shape[0], PART_ROWS)
        for q in range(source.shape[0] // rows):
            at = pl.ds(q * rows, rows)
            loads.append(pltpu.make_async_copy(source.at[at], middle.at[at], load_sem.at[k, q]))
            stores.append(pltpu.make_async_copy(middle.at[at], target.at[at], store_sem.at[k, q]))
    for load in loads:
        load.start()
    for load, store in zip(loads, stores):
        load.wait()
        store.start()
    for store in stores:
        store.wait()


def per_device(out_gate, key_proj, value_proj, residue, log_decay, skip, gain, cotangent):
    length, channels = out_gate.shape
    groups, modes = residue.shape
    members = channels // groups
    ctx_count, tp_count = lax.axis_size("ctx"), lax.axis_size("tp")
    blocks = channels // LANES
    in_block = LANES // members
    subs = length // SUB
    wide = in_block * SUB
    piece_rows = blocks * modes // ctx_count
    pieces = pltpu.VMEM((ctx_count, piece_rows, LANES), F32)
    wide_out = jax.ShapeDtypeStruct((length, channels), BF16)
    table_out = jax.ShapeDtypeStruct((modes, groups), F32)
    hbm = pl.BlockSpec(memory_space=pltpu.HBM)
    results = [wide_out] * 4 + [table_out] * 2
    computed = pl.pallas_call(
        functools.partial(kernel, ctx_count, tp_count, float(channels * tp_count)),
        out_shape=results,
        in_specs=[hbm] * 8,
        out_specs=[hbm] * 6,
        scratch_shapes=[
            pltpu.VMEM((length, channels), BF16),
            pltpu.VMEM((length, channels), BF16),
            pltpu.VMEM((length, channels), BF16),
            pltpu.VMEM((length, channels), BF16),
            pltpu.VMEM((1, channels), F32),
            pltpu.VMEM((1, channels), F32),
            pltpu.VMEM((modes, groups), F32),
            pltpu.VMEM((modes, groups), F32),
            pltpu.VMEM((length, channels), BF16),
            pltpu.VMEM((length, channels), BF16),
            pltpu.VMEM((length, channels), BF16),
            pltpu.VMEM((length, channels), BF16),
            pltpu.VMEM((2 * modes, groups), F32),
            pltpu.VMEM((length, channels), F32),
            pltpu.VMEM((length, channels), F32),
            pltpu.VMEM((length, channels), F32),
            pltpu.VMEM((blocks, 2 * modes, subs * LANES), F32),
            pltpu.VMEM((blocks, subs, 2 * modes, LANES), F32),
            pltpu.VMEM((blocks, modes, LANES), F32),
            pltpu.VMEM((wide, LANES), BF16),
            pltpu.VMEM((in_block * modes, LANES), BF16),
            pltpu.VMEM((groups, wide + LANES), BF16),
            pltpu.VMEM((blocks, 2 * modes, wide + LANES), F32),
            pltpu.VMEM((blocks, 2, 2 * modes, wide), BF16),
            pltpu.VMEM((blocks, 2, SUB, wide), BF16),
            pltpu.VMEM((blocks, 2, SUB, subs * LANES), BF16),
            pltpu.VMEM((blocks, 2 * modes, wide), F32),
            pltpu.VMEM((blocks, 2 * modes, LANES), F32),
            pltpu.VMEM((2, blocks, LANES), F32),
            pltpu.VMEM((2, length, LANES), F32),
            pieces, pieces, pieces, pieces,
            pieces, pieces, pieces, pieces,
            pltpu.VMEM((8, length), F32),
            pltpu.VMEM((tp_count, 8, length), F32),
            pltpu.VMEM((2 * modes, groups), F32),
            pltpu.VMEM((ctx_count, 2 * modes, groups), F32),
            pltpu.SemaphoreType.DMA((5, ctx_count)),
            pltpu.SemaphoreType.DMA((5, ctx_count)),
            pltpu.SemaphoreType.DMA((tp_count,)),
            pltpu.SemaphoreType.DMA((tp_count,)),
            pltpu.SemaphoreType.DMA((8,)),
            pltpu.SemaphoreType.DMA((4,)),
            pltpu.SemaphoreType.DMA((2, blocks)),
        ],
        compiler_params=pltpu.CompilerParams(
            collective_id=0, has_side_effects=True, vmem_limit_bytes=60 * 1024 * 1024
        ),
        name="mixer",
    )(out_gate, key_proj, value_proj, cotangent, skip[None], gain[None], residue.T, log_decay.T)
    *wide_results, grad_residue, grad_log_decay = pl.pallas_call(
        finish,
        out_shape=results,
        in_specs=[hbm] * 6,
        out_specs=[hbm] * 6,
        scratch_shapes=[pltpu.VMEM(result.shape, result.dtype) for result in results]
        + [pltpu.SemaphoreType.DMA((6, length // PART_ROWS))] * 2,
        compiler_params=pltpu.CompilerParams(vmem_limit_bytes=60 * 1024 * 1024),
        name="finish",
    )(*computed)
    return *wide_results, grad_residue.T, grad_log_decay.T


def solution(mesh):
    wide, table, row = P("ctx", "tp"), P("tp", None), P("tp")
    return jax.shard_map(
        per_device,
        mesh=mesh,
        in_specs=(wide, wide, wide, table, table, row, row, wide),
        out_specs=(wide, wide, wide, wide, table, table),
        check_vma=False,
    )
```
